128 devices in a mesh: section: 2 (over x_lo), ctx: 16 (over x_hi, y, core), fsdp: 4 (over z).
Axes of the slice: x: 4 (x_hi: 2, x_lo: 2; x = x_hi * 2 + x_lo), y: 4, z: 4, core: 2. Of those that a mesh axis runs over, the one named last changes fastest.
Arguments:
- ends: bfloat16 [2, 2, 4, 1024, 768], P('section', None, 'fsdp', 'ctx'), may hold values from -6 to 6
- blocks: int32 [2, 32], replicated, may hold values from 0 to 31, as said below
- ln1_gain: bfloat16 [4, 768], P('section', 'fsdp'), may hold values from 0.5 to 1.5
- ln1_bias: bfloat16 [4, 768], P('section', 'fsdp'), may hold values from -3 to 3
- ln2_gain: bfloat16 [4, 768], P('section', 'fsdp'), may hold values from 0.5 to 1.5
- ln2_bias: bfloat16 [4, 768], P('section', 'fsdp'), may hold values from -3 to 3
- qkv_weight: bfloat16 [4, 768, 2304], P('section', 'fsdp'), may hold values from -0.3125 to 0.3125
- qkv_bias: bfloat16 [4, 2304], P('section', 'fsdp'), may hold values from -3 to 3
- out_weight: bfloat16 [4, 768, 768], P('section', 'fsdp'), may hold values from -0.875 to 0.875
- out_bias: bfloat16 [4, 768], P('section', 'fsdp'), may hold values from -3 to 3
- up_weight: bfloat16 [4, 768, 3072], P('section', 'fsdp'), may hold values from -0.21875 to 0.21875
- up_bias: bfloat16 [4, 3072], P('section', 'fsdp'), may hold values from -3 to 3
- down_weight: bfloat16 [4, 3072, 768], P('section', 'fsdp'), may hold values from -0.109375 to 0.109375
- down_bias: bfloat16 [4, 768], P('section', 'fsdp'), may hold values from -3 to 3
Outputs:
- boundary: float32 [2, 2, 4, 1024, 768], P('section', None, 'fsdp', 'ctx')
- grad_ln1_gain: float32 [4, 768], P('section', 'fsdp')
- grad_ln1_bias: float32 [4, 768], P('section', 'fsdp')
- grad_ln2_gain: float32 [4, 768], P('section', 'fsdp')
- grad_ln2_bias: float32 [4, 768], P('section', 'fsdp')
- grad_qkv_weight: float32 [4, 768, 2304], P('section', 'fsdp')
- grad_qkv_bias: float32 [4, 2304], P('section', 'fsdp')
- grad_out_weight: float32 [4, 768, 768], P('section', 'fsdp')
- grad_out_bias: float32 [4, 768], P('section', 'fsdp')
- grad_up_weight: float32 [4, 768, 3072], P('section', 'fsdp')
- grad_up_bias: float32 [4, 3072], P('section', 'fsdp')
- grad_down_weight: float32 [4, 3072, 768], P('section', 'fsdp')
- grad_down_bias: float32 [4, 768], P('section', 'fsdp')
The draws below stay inside these ranges and needn't reach their ends.
Inputs may be any that keep to these rules, and one draw needn't show every extreme that they name: `blocks`: each row holds every number below 32 once; entries 2 c and 2 c + 1 are j and 31 - j for some j, in either order.
All inputs are finite; a program needn't handle non-finite values.
Results may differ from the reference program's by a relative error of at most 0.024.
Values may be sent and summed in bfloat16 or wider, within the bound.
No kernel may reach another device: no remote copies, remote signals or barrier semaphores. Data moves between devices by JAX's collectives and lax.ppermute only.
A program may use at most 320 MiB of HBM per device.

```python
import jax
import jax.numpy as jnp
from jax import lax

D = 768
H = 12
HD = 64
FF = 3072
ROT = 16
SECTION_LAYERS = 2
MB = 2
SEQ_LEN = 1024
LAYERS = 4
SEQS = 4
BLOCKS = 32
BLK = 32


def draw_blocks(key, part):
    key = jax.random.fold_in(key, 7)
    table_rows = []
    for micro_index in range(MB):
        sub_key = jax.random.fold_in(key, micro_index)
        paired = jax.random.permutation(jax.random.fold_in(sub_key, 1), BLOCKS // 2)
        flipped = jax.random.randint(jax.random.fold_in(sub_key, 2), (BLOCKS // 2,), 0, 2)
        lower_half = jnp.where(flipped == 1, BLOCKS - 1 - paired, paired)
        upper_half = BLOCKS - 1 - lower_half
        table_rows.append(jnp.stack([lower_half, upper_half], 1).reshape(BLOCKS))
    return jnp.stack(table_rows).astype(jnp.int32)


def steps_of(rng, dims, shards, least, top_value):
    gain, own = 1.0, jax.random.fold_in(rng, 6)
    for position, parts in shards:
        heights = jnp.exp(jax.random.uniform(jax.random.fold_in(own, position), (parts,), jnp.float32, least / len(shards), top_value / len(shards)))
        gain = gain * jnp.repeat(heights, dims[position] // parts).reshape([-1 if axis == position else 1 for axis in range(len(dims))])
    return gain


def gaussian(stream_key, shape, deviation, limit, shards=(), held_as=jnp.bfloat16):
    result = deviation * jax.random.normal(stream_key, shape, jnp.float32)
    if shards:
        result = result * steps_of(stream_key, shape, shards, -0.22, 0.18)
    return jnp.clip(result, -limit, limit).astype(held_as)


def setup_inputs(seed: int = 0) -> dict:
    streams_of = jax.random.split(jax.random.key(seed), 15)
    return {
        "ends": gaussian(streams_of[0], (2, MB, SEQS, SEQ_LEN, D), 1.0, 6.0, ((0, 2), (2, 4), (3, 16))),
        "blocks": draw_blocks(jax.random.fold_in(streams_of[14], 71), 0),
        "ln1_gain": jnp.clip(1.0 + 0.1 * jax.random.normal(streams_of[2], (LAYERS, D), jnp.float32), 0.5, 1.5).astype(jnp.bfloat16),
        "ln1_bias": gaussian(streams_of[3], (LAYERS, D), 0.5, 3.0, ((0, 2), (1, 4))),
        "ln2_gain": jnp.clip(1.0 + 0.1 * jax.random.normal(streams_of[4], (LAYERS, D), jnp.float32), 0.5, 1.5).astype(jnp.bfloat16),
        "ln2_bias": gaussian(streams_of[5], (LAYERS, D), 0.5, 3.0, ((0, 2), (1, 4))),
        "qkv_weight": gaussian(streams_of[6], (LAYERS, D, 3 * D), (D // 2) ** -0.5, 0.3125, ((0, 2), (1, 4))),
        "qkv_bias": gaussian(streams_of[7], (LAYERS, 3 * D), 0.5, 3.0, ((0, 2), (1, 4))),
        "out_weight": gaussian(streams_of[8], (LAYERS, D, D), (D // 16) ** -0.5, 0.875, ((0, 2), (1, 4))),
        "out_bias": gaussian(streams_of[9], (LAYERS, D), 0.5, 3.0, ((0, 2), (1, 4))),
        "up_weight": gaussian(streams_of[10], (LAYERS, D, FF), D ** -0.5, 0.21875, ((0, 2), (1, 4))),
        "up_bias": gaussian(streams_of[11], (LAYERS, FF), 0.5, 3.0, ((0, 2), (1, 4))),
        "down_weight": gaussian(streams_of[12], (LAYERS, FF, D), FF ** -0.5, 0.109375, ((0, 2), (1, 4))),
        "down_bias": gaussian(streams_of[13], (LAYERS, D), 0.5, 3.0, ((0, 2), (1, 4))),
    }


EPSILON = 1e-05
SCORE_SCALE = 0.125

@jax.custom_vjp
def low(v):
    return lax.optimization_barrier(v.astype(jnp.bfloat16)).astype(jnp.float32)

@jax.custom_vjp
def low_back(v):
    return v

def low_keep(v):
    return (low(v), None)

def low_pass(kept, grad):
    return (grad,)

def back_keep(v):
    return (v, None)

def back_low(kept, grad):
    return (low(grad),)
low.defvjp(low_keep, low_pass)
low_back.defvjp(back_keep, back_low)

def layer_norm(values, gain_vec, shift_vec):
    center = lax.optimization_barrier(jnp.mean(values, -1, keepdims=True))
    offset = values - center
    spread = lax.optimization_barrier(jnp.mean(offset * offset, -1, keepdims=True))
    return offset * lax.rsqrt(spread + EPSILON) * gain_vec + shift_vec

def rotate(head_values, places):
    half_rot = ROT // 2
    frequencies = 10000.0 ** (-jnp.arange(half_rot, dtype=jnp.float32) * 2.0 / ROT)
    angles = places.astype(jnp.float32)[:, None] * frequencies[None, :]
    cosine = jnp.concatenate([jnp.cos(angles), jnp.cos(angles)], -1)[:, None, :]
    sine_table = jnp.concatenate([jnp.sin(angles), jnp.sin(angles)], -1)[:, None, :]
    turned = head_values[..., :ROT]
    swapped = jnp.concatenate([-turned[..., half_rot:], turned[..., :half_rot]], -1)
    return jnp.concatenate([turned * cosine + swapped * sine_table, head_values[..., ROT:]], -1)

def exact_matmul(left_side, right_side):
    return jnp.dot(left_side, right_side, precision=lax.Precision.HIGHEST)

def attend(queries, key_heads, value_heads, query_places, key_places):
    scores = jnp.einsum('qhd,khd->hqk', queries, key_heads, precision=lax.Precision.HIGHEST) * SCORE_SCALE
    scores = low_back(scores)
    scores = jnp.where(query_places[None, :, None] >= key_places[None, None, :], scores, -1e+30)
    row_max = lax.optimization_barrier(jnp.max(scores, -1, keepdims=True))
    raised = jnp.exp(scores - row_max)
    softmax_probs = low(raised / lax.optimization_barrier(jnp.sum(raised, -1, keepdims=True)))
    return jnp.einsum('hqk,khd->qhd', softmax_probs, value_heads, precision=lax.Precision.HIGHEST)

def layer(hidden, places, weights):
    gain_one, shift_one, gain_two, shift_two, w_qkv, b_qkv, w_out, b_out, w_up, b_up, w_down, b_down = weights
    length = hidden.shape[0]
    normed_one = low(layer_norm(hidden, gain_one, shift_one))
    normed_two = low(layer_norm(hidden, gain_two, shift_two))
    merged_proj = low_back(exact_matmul(normed_one, w_qkv) + b_qkv)
    queries = low(rotate(merged_proj[:, :D].reshape(length, H, HD), places))
    key_heads = low(rotate(merged_proj[:, D:2 * D].reshape(length, H, HD), places))
    value_heads = low(merged_proj[:, 2 * D:].reshape(length, H, HD))
    rows_block = min(512, length)
    grouped_queries = queries.reshape(length // rows_block, rows_block, H, HD)
    grouped_places = places.reshape(length // rows_block, rows_block)
    attended = lax.map(jax.checkpoint(lambda item_pair: attend(item_pair[0], key_heads, value_heads, item_pair[1], places)), (grouped_queries, grouped_places))
    attended = low_back(low(attended.reshape(length, D)))
    pre_gelu = low_back(exact_matmul(normed_two, w_up) + b_up)
    activated = low(jax.nn.gelu(pre_gelu, approximate=False))
    branches = exact_matmul(attended, w_out) + b_out + exact_matmul(activated, w_down) + b_down
    return hidden + low_back(branches)

def run_sequence(weights, hidden, places):
    for layer_index in range(LAYERS):
        hidden = layer(hidden, places, tuple((member[layer_index] for member in weights)))
        if (layer_index + 1) % SECTION_LAYERS == 0 and layer_index + 1 < LAYERS:
            hidden = low_back(low(hidden))
    return hidden

def reference(ends, blocks, ln1_gain, ln1_bias, ln2_gain, ln2_bias, qkv_weight, qkv_bias, out_weight, out_bias, up_weight, up_bias, down_weight, down_bias):
    weights = tuple((member.astype(jnp.float32) for member in (ln1_gain, ln1_bias, ln2_gain, ln2_bias, qkv_weight, qkv_bias, out_weight, out_bias, up_weight, up_bias, down_weight, down_bias)))
    starts = ends[0].astype(jnp.float32).reshape(MB * SEQS, SEQ_LEN, D)
    cotangent = ends[1].astype(jnp.float32).reshape(MB * SEQS, SEQ_LEN, D)
    offsets = jnp.arange(SEQ_LEN, dtype=jnp.int32)
    places = blocks[:, offsets // BLK] * BLK + offsets % BLK
    places = jnp.repeat(places, SEQS, axis=0).astype(jnp.int32)

    def forward(params, inputs):
        seq_step = jax.checkpoint(lambda item_pair: run_sequence(params, item_pair[0], item_pair[1]))
        return lax.map(seq_step, (inputs, places))
    final_acts, pull_back = jax.vjp(forward, weights, starts)
    param_grads, input_grads = pull_back(cotangent)
    boundary = jnp.stack([input_grads, final_acts]).reshape(2, MB, SEQS, SEQ_LEN, D)
    return (boundary, param_grads[0], param_grads[1], param_grads[2], param_grads[3], param_grads[4], param_grads[5], param_grads[6], param_grads[7], param_grads[8], param_grads[9], param_grads[10], param_grads[11])
```

```python
import functools

import jax
import jax.numpy as jnp
from jax import lax
from jax.experimental import pallas as pl
from jax.experimental.pallas import tpu as pltpu
from jax.sharding import Mesh, PartitionSpec as P

D = 768
H = 12
HD = 64
FF = 3072
ROT = 16
LAYERS = 4
EPSILON = 1e-05
SCORE_SCALE = 0.125
CHIPS = ("xh", "y")
CTX = ("xh", "y", "c")
EVERY = ("s", "xh", "y", "c", "z")
BF = jnp.bfloat16
F32 = jnp.float32
ROWS = 64
SEQ = 1024
HALF = SEQ // 2
BLOCK = 256
UNITS = 192
SHARE = 416
PACK = 432
VMEM = pltpu.VMEM
ROOM = 56 * 1024 * 1024


def shifted(block, axis, distance):
    size = lax.axis_size(axis)
    return lax.ppermute(block, axis, [(i, (i + distance) % size) for i in range(size)])


def dot(left, right, left_dim=1, right_dim=0):
    return lax.dot_general(
        left, right, (((left_dim,), (right_dim,)), ((), ())), preferred_element_type=F32
    )


def call(kernel, outs, *args, scratch=(), smem=0):
    specs = [pl.BlockSpec(memory_space=pltpu.SMEM)] * smem
    specs += [pl.BlockSpec(memory_space=VMEM)] * (len(args) - smem)
    return pl.pallas_call(
        kernel,
        out_shape=[jax.ShapeDtypeStruct(shape, dtype) for shape, dtype in outs],
        in_specs=specs,
        out_specs=[pl.BlockSpec(memory_space=VMEM)] * len(outs),
        scratch_shapes=list(scratch),
        compiler_params=pltpu.CompilerParams(vmem_limit_bytes=ROOM),
    )(*args)


def centred(x):
    offset = x - jnp.mean(x, -1, keepdims=True)
    scale = lax.rsqrt(jnp.mean(offset * offset, -1, keepdims=True) + EPSILON)
    return offset * scale, scale


def start_kernel(x, n_out):
    n = centred(x[...])[0].astype(BF)
    for k in range(8):
        n_out[k] = n


def finish_kernel(rounded, got, x, bias, x_out, n_out):
    total = got[0].astype(F32)
    for k in range(1, 8):
        total = total + got[k].astype(F32)
    x_next = x[...] + (total + bias[...])
    if rounded:
        x_next = x_next.astype(BF).astype(F32)
    x_out[...] = x_next
    n = centred(x_next)[0].astype(BF)
    for k in range(8):
        n_out[k] = n


def finish_back_kernel(rounded, got, x, dx, dx_out, branch_out):
    gy = got[0].astype(F32)
    for k in range(1, 8):
        gy = gy + got[k].astype(F32)
    n, scale = centred(x[...])
    inner = jnp.mean(gy * n, -1, keepdims=True)
    dx_next = dx[...] + scale * (gy - jnp.mean(gy, -1, keepdims=True) - n * inner)
    if rounded:
        dx_next = dx_next.astype(BF).astype(F32)
    dx_out[...] = dx_next
    branch = dx_next.astype(BF)
    for k in range(8):
        branch_out[k] = branch


def share_weights(owner, share, w_qkv, w_up, w_down, w_out):
    for z in range(4):
        w_qkv[pl.ds(z * 192, 192), :] = share[z, 0:192, 0:192]
        w_up[pl.ds(z * 192, 192), :] = share[z, 0:192, 192:384]
        w_down[pl.ds(z * 48, 48), 0:384] = share[z, 192:240, :]
        w_down[pl.ds(z * 48, 48), 384:768] = share[z, 304:352, :]
    at = owner[0]
    w_out[:, 0:384] = share[at, 240:304, :]
    w_out[:, 384:768] = share[at, 352:416, :]


WEIGHT_SCRATCH = (
    VMEM((D, UNITS), BF),
    VMEM((D, UNITS), BF),
    VMEM((UNITS, D), BF),
    VMEM((HD, D), BF),
)


def scored(q, k, query_places, key_places):
    scores = dot(q, k, 1, 1) * SCORE_SCALE
    scores = jnp.where(query_places >= key_places, scores, -1e30)
    raised = jnp.exp(scores - jnp.max(scores, -1, keepdims=True))
    return raised / jnp.sum(raised, -1, keepdims=True)


def turn(v, tables, rows, sign):
    cosine, ahead, behind = tables
    return v * cosine[rows, :] + sign * (
        pltpu.roll(v, 120, 1) * ahead[rows, :] + pltpu.roll(v, 8, 1) * behind[rows, :]
    )


def forward_kernel(
    owner, own, other, vec, bias, share, cosine, ahead, behind, p_col, p_row,
    part_own, part_other, qkv, pre, act,
    w_qkv, w_up, w_down, w_out,
):
    share_weights(owner, share, w_qkv, w_up, w_down, w_out)
    tables = (cosine, ahead, behind)
    for half, source in enumerate((own, other)):

        @pl.loop(0, HALF // BLOCK)
        def _(step):
            here = pl.ds(step * BLOCK, BLOCK)
            rows = pl.ds(half * HALF + step * BLOCK, BLOCK)
            n = source[here, :].astype(F32)
            one = (n * vec[0:1, :] + vec[1:2, :]).astype(BF)
            two = (n * vec[2:3, :] + vec[3:4, :]).astype(BF)
            merged = dot(one, w_qkv[...]) + bias[0:1, 0:192]
            qkv[rows, 0:128] = turn(merged[:, 0:128], tables, rows, 1.0).astype(BF)
            qkv[rows, 128:192] = merged[:, 128:192].astype(BF)
            up = dot(two, w_up[...]) + bias[1:2, 0:192]
            pre[rows, :] = up
            act[rows, 0:192] = (0.5 * up * (1.0 + lax.erf(up * 0.7071067811865476))).astype(BF)

    k, v = qkv[:, 64:128], qkv[:, 128:192]
    for half, target in enumerate((part_own, part_other)):

        @pl.loop(0, HALF // BLOCK)
        def _(step):
            here = pl.ds(step * BLOCK, BLOCK)
            rows = pl.ds(half * HALF + step * BLOCK, BLOCK)
            probs = scored(qkv[rows, 0:64], k, p_col[rows, :], p_row[...]).astype(BF)
            attended = dot(probs, v).astype(BF)
            act[rows, 192:256] = attended
            part = dot(attended, w_out[...]) + dot(act[rows, 0:192], w_down[...])
            target[here, :] = part.astype(BF)


def backward_kernel(
    owner, b_own, b_other, n_own, n_other, vec, share, cosine, ahead, behind, p_col, p_row, qkv, pre,
    gy_own, gy_other, d_qkv, d_up, sums,
    w_qkv, w_up, w_down, w_out, dq, dk, dv,
):
    share_weights(owner, share, w_qkv, w_up, w_down, w_out)
    tables = (cosine, ahead, behind)
    dk[...] = jnp.zeros_like(dk)
    dv[...] = jnp.zeros_like(dv)
    sums[...] = jnp.zeros_like(sums)
    k, v = qkv[:, 64:128], qkv[:, 128:192]
    for half, source in enumerate((b_own, b_other)):

        @pl.loop(0, HALF // BLOCK)
        def _(step):
            rows = pl.ds(half * HALF + step * BLOCK, BLOCK)
            branch = source[pl.ds(step * BLOCK, BLOCK), :]
            sums[5:6, :] += jnp.sum(branch.astype(F32), 0, keepdims=True)
            hidden = dot(branch, w_down[...], 1, 1)
            up = pre[rows, :]
            slope = 0.5 * (1.0 + lax.erf(up * 0.7071067811865476)) + up * (
                jnp.exp(-0.5 * up * up) * 0.3989422804014327
            )
            d_up[rows, :] = (slope * hidden).astype(BF)
            grad = dot(branch, w_out[...], 1, 1).astype(BF)
            q = qkv[rows, 0:64]
            probs = scored(q, k, p_col[rows, :], p_row[...])
            prob_grad = dot(grad, v, 1, 1)
            inner = jnp.sum(probs * prob_grad, -1, keepdims=True)
            score_grad = (probs * (prob_grad - inner)).astype(BF)
            dq[rows, :] = dot(score_grad, k)
            dk[...] += dot(score_grad, q, 0, 0)
            dv[...] += dot(probs.astype(BF), grad, 0, 0)

    for half, (source, target) in enumerate(((n_own, gy_own), (n_other, gy_other))):

        @pl.loop(0, HALF // BLOCK)
        def _(step):
            here = pl.ds(step * BLOCK, BLOCK)
            rows = pl.ds(half * HALF + step * BLOCK, BLOCK)
            both = jnp.concatenate([dq[rows, :], dk[rows, :]], 1) * SCORE_SCALE
            d_qkv[rows, 0:128] = turn(both, tables, rows, -1.0).astype(BF)
            d_qkv[rows, 128:192] = dv[rows, :].astype(BF)
            g_qkv, g_up = d_qkv[rows, :], d_up[rows, :]
            one = dot(g_qkv, w_qkv[...], 1, 1)
            two = dot(g_up, w_up[...], 1, 1)
            target[here, :] = (one * vec[0:1, :] + two * vec[2:3, :]).astype(BF)
            n = source[here, :].astype(F32)
            for at, part in enumerate((one * n, one, two * n, two)):
                sums[at : at + 1, :] += jnp.sum(part, 0, keepdims=True)
            sums[4:5, 0:192] += jnp.sum(g_qkv.astype(F32), 0, keepdims=True)
            sums[6:7, 0:192] += jnp.sum(g_up.astype(F32), 0, keepdims=True)


def product_kernel(b_own, b_other, n_own, n_other, vec, act, d_qkv, d_up, sums, pack, in_qkv, in_up, in_act):
    in_qkv[...] = jnp.zeros_like(in_qkv)
    in_up[...] = jnp.zeros_like(in_up)
    in_act[...] = jnp.zeros_like(in_act)
    for half, (branch, normal) in enumerate(((b_own, n_own), (b_other, n_other))):

        @pl.loop(0, HALF // BLOCK)
        def _(step):
            here = pl.ds(step * BLOCK, BLOCK)
            rows = pl.ds(half * HALF + step * BLOCK, BLOCK)
            n = normal[here, :].astype(F32)
            one = (n * vec[0:1, :] + vec[1:2, :]).astype(BF)
            two = (n * vec[2:3, :] + vec[3:4, :]).astype(BF)
            in_qkv[...] += dot(one, d_qkv[rows, :], 0, 0)
            in_up[...] += dot(two, d_up[rows, :], 0, 0)
            in_act[...] += dot(act[rows, :], branch[here, :], 0, 0)

    blank = jnp.zeros((12, 384), F32)
    out = in_act[192:256, :].astype(BF)
    for z in range(4):
        pack[z, 0:192, 0:192] = in_qkv[z * 192 : (z + 1) * 192, :].astype(BF)
        pack[z, 0:192, 192:384] = in_up[z * 192 : (z + 1) * 192, :].astype(BF)
        down = in_act[z * 48 : (z + 1) * 48, :].astype(BF)
        pack[z, 192:240, :] = down[:, 0:384]
        pack[z, 240:304, :] = out[:, 0:384]
        pack[z, 304:352, :] = down[:, 384:768]
        pack[z, 352:416, :] = out[:, 384:768]
        cut = sums[:, z * 192 : (z + 1) * 192]
        left = jnp.concatenate([cut[0:1], cut[2:3], sums[4:5, 0:192], cut[5:6]], 0)
        right = jnp.concatenate([cut[1:2], cut[3:4], sums[6:7, 0:192], jnp.zeros((1, 192), F32)], 0)
        rows = jnp.concatenate([left, right], 1)
        pack[z, 416:432, :] = jnp.concatenate([rows, blank], 0).astype(BF)


def unpack_kernel(place, own_a, other_a, own_b, other_b, g_qkv, g_out, g_up, g_down, rest):
    low = place[0] == 0
    z = place[1]
    for j, (own, other) in enumerate(((own_a, other_a), (own_b, other_b))):
        for i in range(16):
            k = i // 2
            mine, theirs = (own, other) if i % 2 == 0 else (other, own)
            block = jnp.where(low, mine[k].astype(F32), theirs[k].astype(F32))
            if i < H:
                for t in range(3):
                    g_qkv[j, :, t * D + i * HD : t * D + (i + 1) * HD] = block[0:192, t * HD : (t + 1) * HD]
            for t in range(4):
                at = t * D + i * 48
                g_up[j, :, at : at + 48] = block[0:192, 192 + t * 48 : 240 + t * 48]
            g_down[j, i * 48 : (i + 1) * 48, 0:384] = block[192:240, :]
            g_down[j, i * 48 : (i + 1) * 48, 384:768] = block[304:352, :]
            rest[j, i] = block[416:432, :]
        for h in range(3):
            i = 3 * z + h
            k = i // 2
            mine = (i % 2) == place[0]
            out = jnp.where(mine, own[k].astype(F32), other[k].astype(F32))
            g_out[j, h * HD : (h + 1) * HD, 0:384] = out[240:304, :]
            g_out[j, h * HD : (h + 1) * HD, 384:768] = out[352:416, :]


def body(ends, blocks, g1, h1, g2, h2, wq, bq, wo, bo, wu, bu, wd, bd):
    s = lax.axis_index("s")
    c = lax.axis_index("c")
    z = lax.axis_index("z")
    first = s == 0
    unit = lax.axis_index(CTX)
    has_head = unit < H
    owner = jnp.minimum(unit // 3, 3).astype(jnp.int32)

    keep = jnp.where(first, ends[0, 0, 0], ends[0, 1, 0])
    received = shifted(jnp.where(first, ends[0, 1, 0], ends[0, 0, 0]), "s", 1)
    x = jnp.where(first, keep, received).astype(F32)
    dx = jnp.where(first, received, keep)

    def from_chips(sent):
        own = lax.all_to_all(sent, CHIPS, 0, 0, tiled=True)
        return own.reshape(HALF, D), shifted(own, "c", 1).reshape(HALF, D)

    def to_chips(own, other):
        part = own + shifted(other, "c", 1)
        return lax.all_to_all(part.reshape(8, ROWS, D), CHIPS, 0, 0, tiled=True)

    n_sent = call(start_kernel, [((8, ROWS, D), BF)], x)[0]
    normals = from_chips(n_sent)

    def share_of(j):
        mask = has_head.astype(BF)
        cols = [lax.dynamic_slice_in_dim(wq[j], t * D + unit * HD, HD, 1) * mask for t in range(3)]
        cols += [lax.dynamic_slice_in_dim(wu[j], t * D + unit * 48, 48, 1) for t in range(4)]
        down = lax.dynamic_slice_in_dim(wd[j], unit * 48, 48, 0)
        out = lax.dynamic_slice_in_dim(wo[j], (unit % 3) * HD, HD, 0) * mask
        rows = jnp.concatenate([down, out], 0)
        return jnp.concatenate([jnp.concatenate(cols, 1), rows[:, :384], rows[:, 384:]], 0)

    def joined_sections(mine):
        theirs = shifted(mine, "s", 1)
        return jnp.where(first, mine, theirs), jnp.where(first, theirs, mine)

    def round_z(block):
        whole = jnp.zeros((4,) + block.shape, BF)
        whole = lax.dynamic_update_slice_in_dim(whole, block[None], z, 0)
        for k in range(1, 4):
            whole = lax.dynamic_update_slice_in_dim(
                whole, shifted(block, "z", k)[None], (z - k) % 4, 0
            )
        return whole

    vectors = jnp.concatenate([g1, h1, g2, h2, bq, bo, bu, bd], 1)
    vectors = round_z(jnp.concatenate(joined_sections(vectors), 0))
    layer_vec, layer_bias, layer_add = [], [], []
    for l in range(LAYERS):
        at, members = 0, []
        for width in (192, 192, 192, 192, 576, 192, 768, 192):
            members.append(vectors[:, l, at : at + width].reshape(1, -1).astype(F32))
            at += width
        layer_vec.append(jnp.concatenate(members[:4] + [jnp.zeros((4, D), F32)], 0))
        head = [lax.dynamic_slice_in_dim(members[4], t * D + unit * HD, HD, 1) for t in range(3)]
        units = [lax.dynamic_slice_in_dim(members[6], t * D + unit * 48, 48, 1) for t in range(4)]
        layer_bias.append(
            jnp.concatenate(
                [jnp.concatenate(head, 1), jnp.concatenate(units, 1), jnp.zeros((6, UNITS), F32)], 0
            )
        )
        layer_add.append(members[5] + members[7])

    early = joined_sections(share_of(0))
    later = joined_sections(share_of(1))
    layer_share = [round_z(early[0])]
    rest = round_z(jnp.stack([later[0], early[1], later[1]]))
    layer_share += [rest[:, i] for i in range(3)]

    blk = ROWS // 2
    offsets = jnp.arange(SEQ, dtype=jnp.int32)
    row_blocks = jnp.where(first, blocks[0], blocks[1])
    places = (jnp.repeat(row_blocks, blk) * blk + offsets % blk).reshape(8, 2, ROWS)
    places = jnp.where(c == 0, places, places[:, ::-1]).transpose(1, 0, 2).reshape(SEQ)
    half = ROT // 2
    frequencies = 10000.0 ** (-jnp.arange(half, dtype=F32) * 2.0 / ROT)
    angles = places.astype(F32)[:, None] * frequencies[None, :]
    cos, sin = jnp.cos(angles), jnp.sin(angles)
    none = jnp.zeros((SEQ, half), F32)
    still = jnp.zeros((SEQ, HD - ROT), F32)
    cosine = jnp.concatenate([cos, cos, still + 1.0] * 2, 1)
    ahead = jnp.concatenate([-sin, none, still] * 2, 1)
    behind = jnp.concatenate([none, sin, still] * 2, 1)
    tables = (cosine, ahead, behind, places[:, None], places[None, :])
    owner = owner.reshape(1)

    kept = []
    for l in range(LAYERS):
        own, other, qkv, pre, act = call(
            forward_kernel,
            [((HALF, D), BF), ((HALF, D), BF), ((SEQ, UNITS), BF), ((SEQ, UNITS), F32), ((SEQ, 256), BF)],
            owner, *normals, layer_vec[l], layer_bias[l], layer_share[l], *tables,
            scratch=WEIGHT_SCRATCH, smem=1,
        )
        kept.append((x, normals, qkv, pre, act))
        got = to_chips(own, other)
        x, n_sent = call(
            functools.partial(finish_kernel, l == 1),
            [((ROWS, D), F32), ((8, ROWS, D), BF)], got, x, layer_add[l],
        )
        if l + 1 < LAYERS:
            normals = from_chips(n_sent)
    final = x

    branches = from_chips(jnp.broadcast_to(dx[None], (8, ROWS, D)))
    dx = dx.astype(F32)
    shares = [None] * LAYERS
    for l in reversed(range(LAYERS)):
        x, normals, qkv, pre, act = kept[l]
        own, other, d_qkv, d_up, sums = call(
            backward_kernel,
            [((HALF, D), BF), ((HALF, D), BF), ((SEQ, UNITS), BF), ((SEQ, UNITS), BF), ((8, D), F32)],
            owner, *branches, *normals, layer_vec[l], layer_share[l], *tables, qkv, pre,
            scratch=WEIGHT_SCRATCH + (VMEM((SEQ, HD), F32),) * 3, smem=1,
        )
        got = to_chips(own, other)
        pack = call(
            product_kernel, [((4, PACK, 384), BF)],
            *branches, *normals, layer_vec[l], act, d_qkv, d_up, sums,
            scratch=(VMEM((D, UNITS), F32), VMEM((D, UNITS), F32), VMEM((256, D), F32)),
        )[0]
        total = lax.dynamic_index_in_dim(pack, z, 0, False).astype(F32)
        for k in range(1, 4):
            sent = lax.dynamic_index_in_dim(pack, (z + k) % 4, 0, False)
            total = total + shifted(sent, "z", k).astype(F32)
        shares[l] = total.astype(BF)
        dx, branch_sent = call(
            functools.partial(finish_back_kernel, l == 2),
            [((ROWS, D), F32), ((8, ROWS, D), BF)], got, x, dx,
        )
        if l > 0:
            branches = from_chips(branch_sent)

    def spread(j):
        mine = jnp.where(first, shares[j], shares[j + 2])
        theirs = shifted(jnp.where(first, shares[j + 2], shares[j]), "s", 1)
        part = (mine.astype(F32) + theirs.astype(F32)).astype(BF)
        sent = jnp.broadcast_to(part[None], (8, PACK, 384))
        own = lax.all_to_all(sent, CHIPS, 0, 0, tiled=True)
        return own, shifted(own, "c", 1)

    second, initial = spread(1), spread(0)
    grad_qkv, grad_out, grad_up, grad_down, extra = call(
        unpack_kernel,
        [((2, 192, 3 * D), F32), ((2, 192, D), F32), ((2, 192, FF), F32), ((2, D, D), F32), ((2, 16, 16, 384), F32)],
        jnp.stack([c, z]).astype(jnp.int32), *initial, *second, smem=1,
    )
    norm_sums = jnp.sum(extra[:, :, 0:2], 1)
    v_g1, v_h1 = norm_sums[:, 0, :192], norm_sums[:, 0, 192:]
    v_g2, v_h2 = norm_sums[:, 1, :192], norm_sums[:, 1, 192:]
    v_qkv = extra[:, :H, 2, :192].reshape(2, H, 3, HD).transpose(0, 2, 1, 3).reshape(2, 3 * D)
    v_qkv = lax.dynamic_slice_in_dim(v_qkv, z * 576, 576, 1)
    v_up = extra[:, :, 2, 192:].reshape(2, 16, 4, 48).transpose(0, 2, 1, 3).reshape(2, 4, D)
    v_up = lax.dynamic_index_in_dim(v_up, z, 1, False)
    v_branch = extra[:, 0, 3, :192]

    came = shifted(jnp.where(first, final, dx), "s", 1)
    have = jnp.where(first, dx, final)
    boundary = jnp.stack([jnp.where(first, have, came), jnp.where(first, came, have)])
    boundary = boundary.reshape(1, 2, 1, ROWS, D)
    return (
        boundary, v_g1, v_h1, v_g2, v_h2, grad_qkv, v_qkv, grad_out, v_branch,
        grad_up, v_up, grad_down, v_branch,
    )


def solution(mesh):
    wide = Mesh(mesh.devices.reshape(2, 2, 4, 2, 4), EVERY)
    acts = P("s", None, "z", CTX, None)
    vec = P("s", "z")
    mat = P("s", "z", None)
    placed = (acts, P(), vec, vec, vec, vec, mat, vec, mat, vec, mat, vec, mat, vec)
    outs = (acts, vec, vec, vec, vec, mat, vec, mat, vec, mat, vec, mat, vec)
    return jax.shard_map(body, mesh=wide, in_specs=placed, out_specs=outs, check_vma=False)
```

```python
import functools

import jax
import jax.numpy as jnp
from jax import lax
from jax.experimental import pallas as pl
from jax.experimental.pallas import tpu as pltpu
from jax.sharding import Mesh, PartitionSpec as P

D = 768
H = 12
HD = 64
FF = 3072
ROT = 16
LAYERS = 4
EPSILON = 1e-05
SCORE_SCALE = 0.125
CHIPS = ("xh", "y")
CTX = ("xh", "y", "c")
EVERY = ("s", "xh", "y", "c", "z")
BF = jnp.bfloat16
F32 = jnp.float32
ROWS = 64
SEQ = 1024
HALF = SEQ // 2
BLOCK = 256
UNITS = 192
SHARE = 416
PACK = 432
VMEM = pltpu.VMEM
MIB = 1024 * 1024


def shifted(block, axis, distance):
    size = lax.axis_size(axis)
    return lax.ppermute(block, axis, [(i, (i + distance) % size) for i in range(size)])


def dot(left, right, left_dim=1, right_dim=0):
    return lax.dot_general(
        left, right, (((left_dim,), (right_dim,)), ((), ())), preferred_element_type=F32
    )


def cost(microseconds):
    return pl.CostEstimate(
        flops=int(microseconds * 1e9), bytes_accessed=int(microseconds * 3.5e6), transcendentals=0
    )


def whole(shape):
    return pl.BlockSpec(shape, lambda _: (0,) * len(shape))


def call(kernel, outs, *args, scratch=(), smem=0, room=12, takes=2):
    specs = [pl.BlockSpec(memory_space=pltpu.SMEM)] * smem
    for i in range(smem, len(args)):
        if isinstance(args[i], tuple):
            block, at = args[i]
            specs.append(pl.BlockSpec((None,) + block.shape[1:], lambda _, at=at: (at, 0, 0)))
        else:
            specs.append(whole(args[i].shape))
    args = [a[0] if isinstance(a, tuple) else a for a in args]
    return pl.pallas_call(
        kernel,
        out_shape=[jax.ShapeDtypeStruct(shape, dtype) for shape, dtype in outs],
        in_specs=specs,
        out_specs=[whole(shape) for shape, _ in outs],
        grid=(1,),
        scratch_shapes=list(scratch),
        cost_estimate=cost(takes),
        compiler_params=pltpu.CompilerParams(vmem_limit_bytes=room * MIB),
    )(*args)


def centred(x):
    offset = x - jnp.mean(x, -1, keepdims=True)
    scale = lax.rsqrt(jnp.mean(offset * offset, -1, keepdims=True) + EPSILON)
    return offset * scale, scale


def start_kernel(x, n_out):
    n = centred(x[...])[0].astype(BF)
    for k in range(8):
        n_out[k] = n


def finish_kernel(rounded, got, x, bias, x_out, n_out):
    total = got[0].astype(F32)
    for k in range(1, 8):
        total = total + got[k].astype(F32)
    x_next = x[...] + (total + bias[...])
    if rounded:
        x_next = x_next.astype(BF).astype(F32)
    x_out[...] = x_next
    n = centred(x_next)[0].astype(BF)
    for k in range(8):
        n_out[k] = n


def finish_back_kernel(rounded, got, x, dx, dx_out, branch_out):
    gy = got[0].astype(F32)
    for k in range(1, 8):
        gy = gy + got[k].astype(F32)
    n, scale = centred(x[...])
    inner = jnp.mean(gy * n, -1, keepdims=True)
    dx_next = dx[...] + scale * (gy - jnp.mean(gy, -1, keepdims=True) - n * inner)
    if rounded:
        dx_next = dx_next.astype(BF).astype(F32)
    dx_out[...] = dx_next
    branch = dx_next.astype(BF)
    for k in range(8):
        branch_out[k] = branch


def share_weights(place, pieces, w_qkv, w_up, w_down, w_out):
    for k, piece in enumerate(pieces):
        at = lax.rem(place[0] + (4 - k), 4)
        w_qkv[pl.ds(pl.multiple_of(at * 192, 64), 192), :] = piece[0:192, 0:192]
        w_up[pl.ds(pl.multiple_of(at * 192, 64), 192), :] = piece[0:192, 192:384]
        w_down[pl.ds(pl.multiple_of(at * 48, 16), 48), 0:384] = piece[192:240, :]
        w_down[pl.ds(pl.multiple_of(at * 48, 16), 48), 384:768] = piece[304:352, :]

        @pl.when(at == place[1])
        def _():
            w_out[:, 0:384] = piece[240:304, :]
            w_out[:, 384:768] = piece[352:416, :]


WEIGHT_SCRATCH = (
    VMEM((D, UNITS), BF),
    VMEM((D, UNITS), BF),
    VMEM((UNITS, D), BF),
    VMEM((HD, D), BF),
)


def scored(q, k, query_places, key_places):
    scores = dot(q * SCORE_SCALE, k, 1, 1)
    scores = jnp.where(query_places >= key_places, scores, -1e30)
    raised = jnp.exp(scores - jnp.max(scores, -1, keepdims=True))
    return raised * (1.0 / jnp.sum(raised, -1, keepdims=True))


def turn(v, tables, rows, sign):
    cosine, ahead, behind = tables
    return v * cosine[rows, :] + sign * (
        pltpu.roll(v, 120, 1) * ahead[rows, :] + pltpu.roll(v, 8, 1) * behind[rows, :]
    )


def forward_kernel(
    place, own, other, vec, bias, s0, s1, s2, s3, cosine, ahead, behind, p_col, p_row,
    part_own, part_other, qkv, pre, act,
    w_qkv, w_up, w_down, w_out,
):
    share_weights(place, (s0, s1, s2, s3), w_qkv, w_up, w_down, w_out)
    tables = (cosine, ahead, behind)
    for half, source in enumerate((own, other)):

        @pl.loop(0, HALF // BLOCK)
        def _(step):
            here = pl.ds(step * BLOCK, BLOCK)
            rows = pl.ds(half * HALF + step * BLOCK, BLOCK)
            n = source[here, :].astype(F32)
            one = (n * vec[0:1, :] + vec[1:2, :]).astype(BF)
            two = (n * vec[2:3, :] + vec[3:4, :]).astype(BF)
            merged = dot(one, w_qkv[...]) + bias[0:1, 0:192]
            qkv[rows, 0:128] = turn(merged[:, 0:128], tables, rows, 1.0).astype(BF)
            qkv[rows, 128:192] = merged[:, 128:192].astype(BF)
            up = dot(two, w_up[...]) + bias[1:2, 0:192]
            pre[rows, :] = up
            act[rows, 0:192] = (0.5 * up * (1.0 + lax.erf(up * 0.7071067811865476))).astype(BF)

    k, v = qkv[:, 64:128], qkv[:, 128:192]
    for half, target in enumerate((part_own, part_other)):

        @pl.loop(0, HALF // BLOCK)
        def _(step):
            here = pl.ds(step * BLOCK, BLOCK)
            rows = pl.ds(half * HALF + step * BLOCK, BLOCK)
            probs = scored(qkv[rows, 0:64], k, p_col[rows, :], p_row[...]).astype(BF)
            attended = dot(probs, v).astype(BF)
            act[rows, 192:256] = attended
            part = dot(attended, w_out[...]) + dot(act[rows, 0:192], w_down[...])
            target[here, :] = part.astype(BF)


def backward_kernel(
    place, b_own, b_other, n_own, n_other, vec, s0, s1, s2, s3, cosine, ahead, behind, p_col, p_row, qkv, pre,
    gy_own, gy_other, d_qkv, d_up, sums,
    w_qkv, w_up, w_down, w_out, dq, dk, dv,
):
    share_weights(place, (s0, s1, s2, s3), w_qkv, w_up, w_down, w_out)
    tables = (cosine, ahead, behind)
    dk[...] = jnp.zeros_like(dk)
    dv[...] = jnp.zeros_like(dv)
    sums[...] = jnp.zeros_like(sums)
    k, v = qkv[:, 64:128], qkv[:, 128:192]
    for half, source in enumerate((b_own, b_other)):

        @pl.loop(0, HALF // BLOCK)
        def _(step):
            rows = pl.ds(half * HALF + step * BLOCK, BLOCK)
            branch = source[pl.ds(step * BLOCK, BLOCK), :]
            sums[5:6, :] += jnp.sum(branch.astype(F32), 0, keepdims=True)
            hidden = dot(branch, w_down[...], 1, 1)
            up = pre[rows, :]
            slope = 0.5 * (1.0 + lax.erf(up * 0.7071067811865476)) + up * (
                jnp.exp(-0.5 * up * up) * 0.3989422804014327
            )
            d_up[rows, :] = (slope * hidden).astype(BF)
            grad = dot(branch, w_out[...], 1, 1).astype(BF)
            q = qkv[rows, 0:64]
            probs = scored(q, k, p_col[rows, :], p_row[...])
            prob_grad = dot(grad, v, 1, 1)
            inner = jnp.sum(probs * prob_grad, -1, keepdims=True)
            score_grad = (probs * (prob_grad - inner)).astype(BF)
            dq[rows, :] = dot(score_grad, k)
            dk[...] += dot(score_grad, q, 0, 0)
            dv[...] += dot(probs.astype(BF), grad, 0, 0)

    for half, (source, target) in enumerate(((n_own, gy_own), (n_other, gy_other))):

        @pl.loop(0, HALF // BLOCK)
        def _(step):
            here = pl.ds(step * BLOCK, BLOCK)
            rows = pl.ds(half * HALF + step * BLOCK, BLOCK)
            both = jnp.concatenate([dq[rows, :], dk[rows, :]], 1) * SCORE_SCALE
            d_qkv[rows, 0:128] = turn(both, tables, rows, -1.0).astype(BF)
            d_qkv[rows, 128:192] = dv[rows, :].astype(BF)
            g_qkv, g_up = d_qkv[rows, :], d_up[rows, :]
            one = dot(g_qkv, w_qkv[...], 1, 1)
            two = dot(g_up, w_up[...], 1, 1)
            target[here, :] = (one * vec[0:1, :] + two * vec[2:3, :]).astype(BF)
            n = source[here, :].astype(F32)
            for at, part in enumerate((one * n, one, two * n, two)):
                sums[at : at + 1, :] += jnp.sum(part, 0, keepdims=True)
            sums[4:5, 0:192] += jnp.sum(g_qkv.astype(F32), 0, keepdims=True)
            sums[6:7, 0:192] += jnp.sum(g_up.astype(F32), 0, keepdims=True)


def product_kernel(b_own, b_other, n_own, n_other, vec, act, d_qkv, d_up, sums, pack, in_qkv, in_up, in_act):
    in_qkv[...] = jnp.zeros_like(in_qkv)
    in_up[...] = jnp.zeros_like(in_up)
    in_act[...] = jnp.zeros_like(in_act)
    for half, (branch, normal) in enumerate(((b_own, n_own), (b_other, n_other))):

        @pl.loop(0, HALF // BLOCK)
        def _(step):
            here = pl.ds(step * BLOCK, BLOCK)
            rows = pl.ds(half * HALF + step * BLOCK, BLOCK)
            n = normal[here, :].astype(F32)
            one = (n * vec[0:1, :] + vec[1:2, :]).astype(BF)
            two = (n * vec[2:3, :] + vec[3:4, :]).astype(BF)
            in_qkv[...] += dot(one, d_qkv[rows, :], 0, 0)
            in_up[...] += dot(two, d_up[rows, :], 0, 0)
            in_act[...] += dot(act[rows, :], branch[here, :], 0, 0)

    blank = jnp.zeros((12, 384), F32)
    out = in_act[192:256, :].astype(BF)
    for z in range(4):
        pack[z, 0:192, 0:192] = in_qkv[z * 192 : (z + 1) * 192, :].astype(BF)
        pack[z, 0:192, 192:384] = in_up[z * 192 : (z + 1) * 192, :].astype(BF)
        down = in_act[z * 48 : (z + 1) * 48, :].astype(BF)
        pack[z, 192:240, :] = down[:, 0:384]
        pack[z, 240:304, :] = out[:, 0:384]
        pack[z, 304:352, :] = down[:, 384:768]
        pack[z, 352:416, :] = out[:, 384:768]
        cut = sums[:, z * 192 : (z + 1) * 192]
        left = jnp.concatenate([cut[0:1], cut[2:3], sums[4:5, 0:192], cut[5:6]], 0)
        right = jnp.concatenate([cut[1:2], cut[3:4], sums[6:7, 0:192], jnp.zeros((1, 192), F32)], 0)
        rows = jnp.concatenate([left, right], 1)
        pack[z, 416:432, :] = jnp.concatenate([rows, blank], 0).astype(BF)


def unpack_kernel(place, own, other, *refs):
    g_qkv, g_out, g_up, g_down, rest = refs[-5:]
    low = place[0] == 0
    z = place[1]
    for i in range(16):
        k = i // 2
        mine, theirs = (own, other) if i % 2 == 0 else (other, own)
        block = jnp.where(low, mine[k], theirs[k]).astype(F32)
        if i < H:
            for t in range(3):
                g_qkv[0, :, t * D + i * HD : t * D + (i + 1) * HD] = block[0:192, t * HD : (t + 1) * HD]
        for t in range(4):
            at = t * D + i * 48
            g_up[0, :, at : at + 48] = block[0:192, 192 + t * 48 : 240 + t * 48]
        g_down[0, i * 48 : (i + 1) * 48, 0:384] = block[192:240, :]
        g_down[0, i * 48 : (i + 1) * 48, 384:768] = block[304:352, :]
        rest[0, i] = block[416:432, :]
    for h in range(3):
        i = 3 * z + h
        k = i // 2
        mine = (i % 2) == place[0]
        out = jnp.where(mine, own[k], other[k]).astype(F32)
        g_out[0, h * HD : (h + 1) * HD, 0:384] = out[240:304, :]
        g_out[0, h * HD : (h + 1) * HD, 384:768] = out[352:416, :]


UNPACKED = ((192, 3 * D), (192, D), (192, FF), (D, D), (16, 16, 384))


def unpacked(j, place, own, other, earlier):
    specs = [pl.BlockSpec(memory_space=pltpu.SMEM)]
    specs += [pl.BlockSpec((8, PACK, 384), lambda i: (0, 0, 0))] * 2
    specs += [pl.BlockSpec(memory_space=pl.ANY)] * len(earlier)
    return pl.pallas_call(
        unpack_kernel,
        grid=(1,),
        out_shape=[jax.ShapeDtypeStruct((2,) + shape, F32) for shape in UNPACKED],
        in_specs=specs,
        out_specs=[
            pl.BlockSpec((1,) + shape, lambda i, n=len(shape): (j,) + (0,) * n) for shape in UNPACKED
        ],
        input_output_aliases={3 + i: i for i in range(len(earlier))},
        cost_estimate=cost(7),
        compiler_params=pltpu.CompilerParams(vmem_limit_bytes=40 * MIB),
    )(place, own, other, *earlier)


def after(earlier, later):
    return lax.optimization_barrier((earlier, later))[1]


def body(ends, blocks, g1, h1, g2, h2, wq, bq, wo, bo, wu, bu, wd, bd):
    s = lax.axis_index("s")
    c = lax.axis_index("c")
    z = lax.axis_index("z")
    first = s == 0
    unit = lax.axis_index(CTX)
    has_head = unit < H
    owner = jnp.minimum(unit // 3, 3).astype(jnp.int32)

    keep = jnp.where(first, ends[0, 0, 0], ends[0, 1, 0])
    received = shifted(jnp.where(first, ends[0, 1, 0], ends[0, 0, 0]), "s", 1)
    x = jnp.where(first, keep, received).astype(F32)
    dx = jnp.where(first, received, keep)

    def exchanged(sent, beside=None):
        got = lax.all_to_all(sent, CHIPS, 0, 0, tiled=True)
        return got if beside is None else lax.optimization_barrier((got, beside))

    def both_cores(own):
        return own.reshape(HALF, D), shifted(own, "c", 1).reshape(HALF, D)

    def halves_joined(own, other):
        return (own + shifted(other, "c", 1)).reshape(8, ROWS, D)

    n_sent = call(start_kernel, [((8, ROWS, D), BF)], x)[0]
    mask = has_head.astype(BF)

    def cut(w, at, sizes):
        return lax.dynamic_slice(w, at, sizes)

    zero = jnp.int32(0)
    cols = [cut(wq, (zero, zero, t * D + unit * HD), (2, 192, HD)) * mask for t in range(3)]
    cols += [cut(wu, (zero, zero, t * D + unit * 48), (2, 192, 48)) for t in range(4)]
    down = cut(wd, (zero, unit * 48, zero), (2, 48, D))
    out = cut(wo, (zero, (unit % 3) * HD, zero), (2, HD, D)) * mask
    rows = jnp.concatenate([down, out], 1)
    shares = jnp.concatenate([jnp.concatenate(cols, 2), rows[..., :384], rows[..., 384:]], 1)

    def joined_sections(mine):
        theirs = shifted(mine, "s", 1)
        return jnp.where(first, mine, theirs), jnp.where(first, theirs, mine)

    def pieces_round_z(block):
        return [block] + [shifted(block, "z", k) for k in range(1, 4)]

    def round_z(block):
        pieces = pieces_round_z(block)
        order = [pieces[0]] * 4
        for at in range(4):
            order[at] = jnp.where(
                z == at,
                pieces[0],
                jnp.where(
                    z == (at + 1) % 4, pieces[1], jnp.where(z == (at + 2) % 4, pieces[2], pieces[3])
                ),
            )
        return jnp.stack(order)

    early = joined_sections(shares[0])
    early = after(n_sent, early)
    layer_share = [[(piece, 0) for piece in pieces_round_z(early[0][None])]]
    later = joined_sections(after(early, shares[1]))

    vectors = after(early, jnp.concatenate([g1, h1, g2, h2, bq, bo, bu, bd], 1))
    vectors = round_z(jnp.concatenate(joined_sections(vectors), 0))
    layer_vec, layer_bias, layer_add = [], [], []
    for l in range(LAYERS):
        at, members = 0, []
        for width in (192, 192, 192, 192, 576, 192, 768, 192):
            members.append(vectors[:, l, at : at + width].reshape(1, -1).astype(F32))
            at += width
        layer_vec.append(jnp.concatenate(members[:4] + [jnp.zeros((4, D), F32)], 0))
        head = [lax.dynamic_slice_in_dim(members[4], t * D + unit * HD, HD, 1) for t in range(3)]
        units = [lax.dynamic_slice_in_dim(members[6], t * D + unit * 48, 48, 1) for t in range(4)]
        layer_bias.append(
            jnp.concatenate(
                [jnp.concatenate(head, 1), jnp.concatenate(units, 1), jnp.zeros((6, UNITS), F32)], 0
            )
        )
        layer_add.append(members[5] + members[7])

    blk = ROWS // 2
    offsets = jnp.arange(SEQ, dtype=jnp.int32)
    blocks = after(early, blocks)
    row_blocks = jnp.where(first, blocks[0], blocks[1])
    places = (jnp.repeat(row_blocks, blk) * blk + offsets % blk).reshape(8, 2, ROWS)
    places = jnp.where(c == 0, places, places[:, ::-1]).transpose(1, 0, 2).reshape(SEQ)
    half = ROT // 2
    frequencies = 10000.0 ** (-jnp.arange(half, dtype=F32) * 2.0 / ROT)
    angles = places.astype(F32)[:, None] * frequencies[None, :]
    cos, sin = jnp.cos(angles), jnp.sin(angles)
    none = jnp.zeros((SEQ, half), F32)
    still = jnp.zeros((SEQ, HD - ROT), F32)
    cosine = jnp.concatenate([cos, cos, still + 1.0] * 2, 1)
    ahead = jnp.concatenate([-sin, none, still] * 2, 1)
    behind = jnp.concatenate([none, sin, still] * 2, 1)
    tables = (cosine, ahead, behind, places[:, None], places[None, :])
    own, (tables, layer_vec, layer_bias, layer_add, layer_share[0]) = exchanged(
        n_sent, (tables, layer_vec, layer_bias, layer_add, [piece for piece, _ in layer_share[0]])
    )
    layer_share[0] = [(piece, 0) for piece in layer_share[0]]
    normals = both_cores(own)
    place = jnp.stack([z.astype(jnp.int32), owner])

    kept = []
    for l in range(LAYERS):
        own, other, qkv, pre, act = call(
            forward_kernel,
            [((HALF, D), BF), ((HALF, D), BF), ((SEQ, UNITS), BF), ((SEQ, UNITS), F32), ((SEQ, 256), BF)],
            place, *normals, layer_vec[l], layer_bias[l], *layer_share[l], *tables,
            scratch=WEIGHT_SCRATCH, smem=1, room=56, takes=11,
        )
        if l == 1:
            sent = after(normals, jnp.broadcast_to(dx[None], (8, ROWS, D)))
            branches, (own, other) = exchanged(sent, (own, other))
            branches = both_cores(branches)
        kept.append((x, normals, qkv, pre, act))
        if l + 1 < LAYERS:
            got = exchanged(halves_joined(own, other))
            x, n_sent = call(
                functools.partial(finish_kernel, l == 1),
                [((ROWS, D), F32), ((8, ROWS, D), BF)], got, x, layer_add[l],
            )
            if l == 0:
                block = after(normals, jnp.stack([later[0], early[1], later[1]]))
                own, pieces = exchanged(n_sent, pieces_round_z(block))
                layer_share += [[(piece, i) for piece in pieces] for i in range(3)]
                normals = both_cores(own)
            else:
                normals = both_cores(exchanged(n_sent))
    last = halves_joined(own, other)

    dx = dx.astype(F32)
    packs, shares = [None] * LAYERS, [None] * LAYERS
    def sent_round(pack):
        parts = [lax.dynamic_index_in_dim(pack, (z + k) % 4, 0, False) for k in range(4)]
        return [parts[0]] + [shifted(parts[k], "z", k) for k in range(1, 4)]

    def summed(parts):
        return sum(part.astype(F32) for part in parts).astype(BF)

    def both_sections(j):
        mine = jnp.where(first, shares[j], shares[j + 2])
        theirs = shifted(jnp.where(first, shares[j + 2], shares[j]), "s", 1)
        return (mine.astype(F32) + theirs.astype(F32)).astype(BF)

    for l in reversed(range(LAYERS)):
        x, normals, qkv, pre, act = kept[l]
        own, other, d_qkv, d_up, sums = call(
            backward_kernel,
            [((HALF, D), BF), ((HALF, D), BF), ((SEQ, UNITS), BF), ((SEQ, UNITS), BF), ((8, D), F32)],
            place, *branches, *normals, layer_vec[l], *layer_share[l], *tables, qkv, pre,
            scratch=WEIGHT_SCRATCH + (VMEM((SEQ, HD), F32),) * 3, smem=1, room=56, takes=13,
        )
        if l + 1 == LAYERS:
            got, (own, other) = exchanged(last, (own, other))
            final = call(
                functools.partial(finish_kernel, False),
                [((ROWS, D), F32), ((8, ROWS, D), BF)], got, x, layer_add[l],
            )[0]
        else:
            own, other, parts = lax.optimization_barrier((own, other, parts))
            shares[l + 1] = summed(parts)
        pack = call(
            product_kernel, [((4, PACK, 384), BF)],
            *branches, *normals, layer_vec[l], act, d_qkv, d_up, sums,
            scratch=(VMEM((D, UNITS), F32), VMEM((D, UNITS), F32), VMEM((256, D), F32)),
            room=56, takes=6,
        )[0]
        got, pack = exchanged(halves_joined(own, other), pack)
        dx, branch_sent = call(
            functools.partial(finish_back_kernel, l == 2),
            [((ROWS, D), F32), ((8, ROWS, D), BF)], got, x, dx,
        )
        if l > 0:
            parts = sent_round(pack)
            branches, parts[2] = exchanged(branch_sent, parts[2])
            branches = both_cores(branches)

    sent = jnp.broadcast_to(after(got, both_sections(1))[None], (8, PACK, 384))
    shares[0] = summed(sent_round(pack))
    own, initial = exchanged(sent, (both_sections(0), dx))
    initial, dx = initial

    corner = jnp.stack([c, z]).astype(jnp.int32)
    earlier = unpacked(1, corner, own, shifted(own, "c", 1), ())
    sent = jnp.broadcast_to(initial[None], (8, PACK, 384))
    came = shifted(jnp.where(first, final, dx), "s", 1)
    own, (earlier, came) = exchanged(sent, (earlier, came))
    grad_qkv, grad_out, grad_up, grad_down, extra = unpacked(
        0, corner, own, shifted(own, "c", 1), earlier
    )
    norm_sums = jnp.sum(extra[:, :, 0:2], 1)
    v_g1, v_h1 = norm_sums[:, 0, :192], norm_sums[:, 0, 192:]
    v_g2, v_h2 = norm_sums[:, 1, :192], norm_sums[:, 1, 192:]
    v_qkv = extra[:, :H, 2, :192].reshape(2, H, 3, HD).transpose(0, 2, 1, 3).reshape(2, 3 * D)
    v_qkv = lax.dynamic_slice_in_dim(v_qkv, z * 576, 576, 1)
    v_up = extra[:, :, 2, 192:].reshape(2, 16, 4, 48).transpose(0, 2, 1, 3).reshape(2, 4, D)
    v_up = lax.dynamic_index_in_dim(v_up, z, 1, False)
    v_branch = extra[:, 0, 3, :192]

    have = jnp.where(first, dx, final)
    boundary = jnp.stack([jnp.where(first, have, came), jnp.where(first, came, have)])
    boundary = boundary.reshape(1, 2, 1, ROWS, D)
    return (
        boundary, v_g1, v_h1, v_g2, v_h2, grad_qkv, v_qkv, grad_out, v_branch,
        grad_up, v_up, grad_down, v_branch,
    )


def solution(mesh):
    wide = Mesh(mesh.devices.reshape(2, 2, 4, 2, 4), EVERY)
    acts = P("s", None, "z", CTX, None)
    vec = P("s", "z")
    mat = P("s", "z", None)
    placed = (acts, P(), vec, vec, vec, vec, mat, vec, mat, vec, mat, vec, mat, vec)
    outs = (acts, vec, vec, vec, vec, mat, vec, mat, vec, mat, vec, mat, vec)
    return jax.shard_map(body, mesh=wide, in_specs=placed, out_specs=outs, check_vma=False)
```

```python
import functools

import jax
import jax.numpy as jnp
from jax import lax
from jax.experimental import pallas as pl
from jax.experimental.pallas import tpu as pltpu
from jax.sharding import Mesh, PartitionSpec as P

D = 768
H = 12
HD = 64
FF = 3072
ROT = 16
LAYERS = 4
EPSILON = 1e-05
SCORE_SCALE = 0.125
CHIPS = ("xh", "y")
CTX = ("xh", "y", "c")
EVERY = ("s", "xh", "y", "c", "z")
BF = jnp.bfloat16
F32 = jnp.float32
ROWS = 64
SEQ = 1024
HALF = SEQ // 2
BLOCK = 256
BLK = 32
UNITS = 192
SHARE = 416
PACK = 432
VMEM = pltpu.VMEM
MIB = 1024 * 1024


def shifted(block, axis, distance):
    size = lax.axis_size(axis)
    return lax.ppermute(block, axis, [(i, (i + distance) % size) for i in range(size)])


def dot(left, right, left_dim=1, right_dim=0):
    return lax.dot_general(
        left, right, (((left_dim,), (right_dim,)), ((), ())), preferred_element_type=F32
    )


def cost(microseconds):
    return pl.CostEstimate(
        flops=int(microseconds * 1e9), bytes_accessed=int(microseconds * 3.5e6), transcendentals=0
    )


def whole(shape):
    return pl.BlockSpec(shape, lambda _: (0,) * len(shape))


def call(kernel, outs, *args, scratch=(), smem=0, room=12, takes=2):
    specs = [pl.BlockSpec(memory_space=pltpu.SMEM)] * smem
    for i in range(smem, len(args)):
        if isinstance(args[i], tuple):
            block, at = args[i]
            specs.append(pl.BlockSpec((None,) + block.shape[1:], lambda _, at=at: (at, 0, 0)))
        else:
            specs.append(whole(args[i].shape))
    args = [a[0] if isinstance(a, tuple) else a for a in args]
    return pl.pallas_call(
        kernel,
        out_shape=[jax.ShapeDtypeStruct(shape, dtype) for shape, dtype in outs],
        in_specs=specs,
        out_specs=[whole(shape) for shape, _ in outs],
        grid=(1,),
        scratch_shapes=list(scratch),
        cost_estimate=cost(takes),
        compiler_params=pltpu.CompilerParams(vmem_limit_bytes=room * MIB),
    )(*args)


def centred(x):
    offset = x - jnp.mean(x, -1, keepdims=True)
    scale = lax.rsqrt(jnp.mean(offset * offset, -1, keepdims=True) + EPSILON)
    return offset * scale, scale


def start_kernel(x, n_out):
    n = centred(x[...])[0].astype(BF)
    for k in range(8):
        n_out[k] = n


def finish_kernel(rounded, got, x, bias, x_out, n_out):
    total = got[0].astype(F32)
    for k in range(1, 8):
        total = total + got[k].astype(F32)
    x_next = x[...] + (total + bias[...])
    if rounded:
        x_next = x_next.astype(BF).astype(F32)
    x_out[...] = x_next
    n = centred(x_next)[0].astype(BF)
    for k in range(8):
        n_out[k] = n


def finish_back_kernel(rounded, got, x, dx, dx_out, branch_out):
    gy = got[0].astype(F32)
    for k in range(1, 8):
        gy = gy + got[k].astype(F32)
    n, scale = centred(x[...])
    inner = jnp.mean(gy * n, -1, keepdims=True)
    dx_next = dx[...] + scale * (gy - jnp.mean(gy, -1, keepdims=True) - n * inner)
    if rounded:
        dx_next = dx_next.astype(BF).astype(F32)
    dx_out[...] = dx_next
    branch = dx_next.astype(BF)
    for k in range(8):
        branch_out[k] = branch


def share_weights(place, pieces, w_qkv, w_up, w_both):
    for k, piece in enumerate(pieces):
        at = lax.rem(place[0] + (4 - k), 4)
        w_qkv[pl.ds(pl.multiple_of(at * 192, 64), 192), :] = piece[0:192, 0:192]
        w_up[pl.ds(pl.multiple_of(at * 192, 64), 192), :] = piece[0:192, 192:384]
        w_both[pl.ds(pl.multiple_of(at * 48, 16), 48), 0:384] = piece[192:240, :]
        w_both[pl.ds(pl.multiple_of(at * 48, 16), 48), 384:768] = piece[304:352, :]

        @pl.when(at == place[1])
        def _():
            w_both[192:256, 0:384] = piece[240:304, :]
            w_both[192:256, 384:768] = piece[352:416, :]


WEIGHT_SCRATCH = (VMEM((D, UNITS), BF), VMEM((D, UNITS), BF), VMEM((UNITS + HD, D), BF))


def scored(tile, q, k):
    scores = dot(q * SCORE_SCALE, k, 1, 1)
    row = lax.broadcasted_iota(jnp.int32, (BLOCK, BLOCK), 0)
    column = lax.broadcasted_iota(jnp.int32, (BLOCK, BLOCK), 1)
    last = jnp.where(row >= column, scores[:, tile * BLOCK :], -1e30)
    if tile:
        last = jnp.concatenate([scores[:, : tile * BLOCK], last], 1)
    raised = jnp.exp(last - jnp.max(last, -1, keepdims=True))
    return raised * (1.0 / jnp.sum(raised, -1, keepdims=True))


def spots(order, half, step):
    for i in range(BLOCK // BLK):
        at = order[half * (HALF // BLK) + step * (BLOCK // BLK) + i]
        yield i * BLK, pl.ds(pl.multiple_of(at * BLK, BLK), BLK)


def turn(v, tables, rows, sign):
    cosine, ahead, behind = tables
    return v * cosine[rows, :] + sign * (
        pltpu.roll(v, 120, 1) * ahead[rows, :] + pltpu.roll(v, 8, 1) * behind[rows, :]
    )


def forward_kernel(
    place, order, own, other, vec, bias, s0, s1, s2, s3, cosine, ahead, behind,
    part_own, part_other, qkv, pre, act,
    w_qkv, w_up, w_both, att,
):
    share_weights(place, (s0, s1, s2, s3), w_qkv, w_up, w_both)
    tables = (cosine, ahead, behind)
    for half, source in enumerate((own, other)):

        @pl.loop(0, HALF // BLOCK)
        def _(step):
            here = pl.ds(step * BLOCK, BLOCK)
            rows = pl.ds(half * HALF + step * BLOCK, BLOCK)
            n = source[here, :].astype(F32)
            one = (n * vec[0:1, :] + vec[1:2, :]).astype(BF)
            two = (n * vec[2:3, :] + vec[3:4, :]).astype(BF)
            merged = dot(one, w_qkv[...]) + bias[0:1, 0:192]
            qk = turn(merged[:, 0:128], tables, rows, 1.0).astype(BF)
            v = merged[:, 128:192].astype(BF)
            for at, spot in spots(order, half, step):
                qkv[spot, 0:128] = qk[at : at + BLK, :]
                qkv[spot, 128:192] = v[at : at + BLK, :]
            up = dot(two, w_up[...]) + bias[1:2, 0:192]
            pre[rows, :] = up
            act[rows, 0:192] = (0.5 * up * (1.0 + lax.erf(up * 0.7071067811865476))).astype(BF)

    for tile in range(SEQ // BLOCK):
        start, end = tile * BLOCK, (tile + 1) * BLOCK
        probs = scored(tile, qkv[start:end, 0:64], qkv[0:end, 64:128]).astype(BF)
        att[start:end, :] = dot(probs, qkv[0:end, 128:192]).astype(BF)

    for half, target in enumerate((part_own, part_other)):

        @pl.loop(0, HALF // BLOCK)
        def _(step):
            rows = pl.ds(half * HALF + step * BLOCK, BLOCK)
            attended = jnp.concatenate([att[spot, :] for _, spot in spots(order, half, step)], 0)
            act[rows, 192:256] = attended
            target[pl.ds(step * BLOCK, BLOCK), :] = dot(act[rows, :], w_both[...]).astype(BF)


def backward_kernel(
    place, order, b_own, b_other, n_own, n_other, vec, s0, s1, s2, s3, cosine, ahead, behind, qkv, pre,
    gy_own, gy_other, d_qkv, d_up, sums,
    w_qkv, w_up, w_both, dq, dk, dv, grad,
):
    share_weights(place, (s0, s1, s2, s3), w_qkv, w_up, w_both)
    tables = (cosine, ahead, behind)
    sums[...] = jnp.zeros_like(sums)
    for half, source in enumerate((b_own, b_other)):

        @pl.loop(0, HALF // BLOCK)
        def _(step):
            rows = pl.ds(half * HALF + step * BLOCK, BLOCK)
            branch = source[pl.ds(step * BLOCK, BLOCK), :]
            sums[5:6, :] += jnp.sum(branch.astype(F32), 0, keepdims=True)
            both = dot(branch, w_both[...], 1, 1)
            up = pre[rows, :]
            slope = 0.5 * (1.0 + lax.erf(up * 0.7071067811865476)) + up * (
                jnp.exp(-0.5 * up * up) * 0.3989422804014327
            )
            d_up[rows, :] = (slope * both[:, 0:192]).astype(BF)
            head = both[:, 192:256].astype(BF)
            for at, spot in spots(order, half, step):
                grad[spot, :] = head[at : at + BLK, :]

    for tile in reversed(range(SEQ // BLOCK)):
        start, end = tile * BLOCK, (tile + 1) * BLOCK
        q, k, v = qkv[start:end, 0:64], qkv[0:end, 64:128], qkv[0:end, 128:192]
        out = grad[start:end, :]
        probs = scored(tile, q, k)
        prob_grad = dot(out, v, 1, 1)
        inner = jnp.sum(probs * prob_grad, -1, keepdims=True)
        score_grad = (probs * (prob_grad - inner)).astype(BF)
        dq[start:end, :] = dot(score_grad, k)
        k_part, v_part = dot(score_grad, q, 0, 0), dot(probs.astype(BF), out, 0, 0)
        if end == SEQ:
            dk[...] = k_part
            dv[...] = v_part
        else:
            dk[0:end, :] += k_part
            dv[0:end, :] += v_part

    for half, (source, target) in enumerate(((n_own, gy_own), (n_other, gy_other))):

        @pl.loop(0, HALF // BLOCK)
        def _(step):
            here = pl.ds(step * BLOCK, BLOCK)
            rows = pl.ds(half * HALF + step * BLOCK, BLOCK)
            places = [spot for _, spot in spots(order, half, step)]
            both = jnp.concatenate(
                [jnp.concatenate([ref[spot, :] for spot in places], 0) for ref in (dq, dk)], 1
            )
            d_qkv[rows, 0:128] = turn(both * SCORE_SCALE, tables, rows, -1.0).astype(BF)
            d_qkv[rows, 128:192] = jnp.concatenate([dv[spot, :] for spot in places], 0).astype(BF)
            g_qkv, g_up = d_qkv[rows, :], d_up[rows, :]
            one = dot(g_qkv, w_qkv[...], 1, 1)
            two = dot(g_up, w_up[...], 1, 1)
            target[here, :] = (one * vec[0:1, :] + two * vec[2:3, :]).astype(BF)
            n = source[here, :].astype(F32)
            for at, part in enumerate((one * n, one, two * n, two)):
                sums[at : at + 1, :] += jnp.sum(part, 0, keepdims=True)
            sums[4:5, 0:192] += jnp.sum(g_qkv.astype(F32), 0, keepdims=True)
            sums[6:7, 0:192] += jnp.sum(g_up.astype(F32), 0, keepdims=True)


def product_kernel(b_own, b_other, n_own, n_other, vec, act, d_qkv, d_up, sums, pack, in_qkv, in_up, in_act):
    in_qkv[...] = jnp.zeros_like(in_qkv)
    in_up[...] = jnp.zeros_like(in_up)
    in_act[...] = jnp.zeros_like(in_act)
    for half, (branch, normal) in enumerate(((b_own, n_own), (b_other, n_other))):

        @pl.loop(0, HALF // BLOCK)
        def _(step):
            here = pl.ds(step * BLOCK, BLOCK)
            rows = pl.ds(half * HALF + step * BLOCK, BLOCK)
            n = normal[here, :].astype(F32)
            one = (n * vec[0:1, :] + vec[1:2, :]).astype(BF)
            two = (n * vec[2:3, :] + vec[3:4, :]).astype(BF)
            in_qkv[...] += dot(one, d_qkv[rows, :], 0, 0)
            in_up[...] += dot(two, d_up[rows, :], 0, 0)
            in_act[...] += dot(act[rows, :], branch[here, :], 0, 0)

    blank = jnp.zeros((12, 384), F32)
    out = in_act[192:256, :].astype(BF)
    for z in range(4):
        pack[z, 0:192, 0:192] = in_qkv[z * 192 : (z + 1) * 192, :].astype(BF)
        pack[z, 0:192, 192:384] = in_up[z * 192 : (z + 1) * 192, :].astype(BF)
        down = in_act[z * 48 : (z + 1) * 48, :].astype(BF)
        pack[z, 192:240, :] = down[:, 0:384]
        pack[z, 240:304, :] = out[:, 0:384]
        pack[z, 304:352, :] = down[:, 384:768]
        pack[z, 352:416, :] = out[:, 384:768]
        cut = sums[:, z * 192 : (z + 1) * 192]
        left = jnp.concatenate([cut[0:1], cut[2:3], sums[4:5, 0:192], cut[5:6]], 0)
        right = jnp.concatenate([cut[1:2], cut[3:4], sums[6:7, 0:192], jnp.zeros((1, 192), F32)], 0)
        rows = jnp.concatenate([left, right], 1)
        pack[z, 416:432, :] = jnp.concatenate([rows, blank], 0).astype(BF)


def unpack_kernel(place, own, other, *refs):
    g_qkv, g_out, g_up, g_down, rest = refs[-5:]
    low = place[0] == 0
    z = place[1]
    for i in range(16):
        k = i // 2
        mine, theirs = (own, other) if i % 2 == 0 else (other, own)
        block = jnp.where(low, mine[k], theirs[k]).astype(F32)
        if i < H:
            for t in range(3):
                g_qkv[0, :, t * D + i * HD : t * D + (i + 1) * HD] = block[0:192, t * HD : (t + 1) * HD]
        for t in range(4):
            at = t * D + i * 48
            g_up[0, :, at : at + 48] = block[0:192, 192 + t * 48 : 240 + t * 48]
        g_down[0, i * 48 : (i + 1) * 48, 0:384] = block[192:240, :]
        g_down[0, i * 48 : (i + 1) * 48, 384:768] = block[304:352, :]
        rest[0, i] = block[416:432, :]
    for h in range(3):
        i = 3 * z + h
        k = i // 2
        mine = (i % 2) == place[0]
        out = jnp.where(mine, own[k], other[k]).astype(F32)
        g_out[0, h * HD : (h + 1) * HD, 0:384] = out[240:304, :]
        g_out[0, h * HD : (h + 1) * HD, 384:768] = out[352:416, :]


UNPACKED = ((192, 3 * D), (192, D), (192, FF), (D, D), (16, 16, 384))


def unpacked(j, place, own, other, earlier):
    specs = [pl.BlockSpec(memory_space=pltpu.SMEM)]
    specs += [pl.BlockSpec((8, PACK, 384), lambda i: (0, 0, 0))] * 2
    specs += [pl.BlockSpec(memory_space=pl.ANY)] * len(earlier)
    return pl.pallas_call(
        unpack_kernel,
        grid=(1,),
        out_shape=[jax.ShapeDtypeStruct((2,) + shape, F32) for shape in UNPACKED],
        in_specs=specs,
        out_specs=[
            pl.BlockSpec((1,) + shape, lambda i, n=len(shape): (j,) + (0,) * n) for shape in UNPACKED
        ],
        input_output_aliases={3 + i: i for i in range(len(earlier))},
        cost_estimate=cost(7),
        compiler_params=pltpu.CompilerParams(vmem_limit_bytes=56 * MIB),
    )(place, own, other, *earlier)


def after(earlier, later):
    return lax.optimization_barrier((earlier, later))[1]


def body(ends, blocks, g1, h1, g2, h2, wq, bq, wo, bo, wu, bu, wd, bd):
    s = lax.axis_index("s")
    c = lax.axis_index("c")
    z = lax.axis_index("z")
    first = s == 0
    unit = lax.axis_index(CTX)
    has_head = unit < H
    owner = jnp.minimum(unit // 3, 3).astype(jnp.int32)

    keep = jnp.where(first, ends[0, 0, 0], ends[0, 1, 0])
    received = shifted(jnp.where(first, ends[0, 1, 0], ends[0, 0, 0]), "s", 1)
    x = jnp.where(first, keep, received).astype(F32)
    dx = jnp.where(first, received, keep)

    def exchanged(sent, beside=None):
        got = lax.all_to_all(sent, CHIPS, 0, 0, tiled=True)
        return got if beside is None else lax.optimization_barrier((got, beside))

    def both_cores(own):
        return own.reshape(HALF, D), shifted(own, "c", 1).reshape(HALF, D)

    def halves_joined(own, other):
        return (own + shifted(other, "c", 1)).reshape(8, ROWS, D)

    n_sent = call(start_kernel, [((8, ROWS, D), BF)], x)[0]
    mask = has_head.astype(BF)

    def cut(w, at, sizes):
        return lax.dynamic_slice(w, at, sizes)

    zero = jnp.int32(0)
    cols = [cut(wq, (zero, zero, t * D + unit * HD), (2, 192, HD)) * mask for t in range(3)]
    cols += [cut(wu, (zero, zero, t * D + unit * 48), (2, 192, 48)) for t in range(4)]
    down = cut(wd, (zero, unit * 48, zero), (2, 48, D))
    out = cut(wo, (zero, (unit % 3) * HD, zero), (2, HD, D)) * mask
    rows = jnp.concatenate([down, out], 1)
    vectors = jnp.concatenate([g1, h1, g2, h2, bq, bo, bu, bd], 1)
    vectors = jnp.pad(vectors, ((0, 0), (0, 16 * 384 - vectors.shape[1]))).reshape(2, 16, 384)
    shares = jnp.concatenate(
        [jnp.concatenate(cols, 2), rows[..., :384], rows[..., 384:], vectors], 1
    )

    def joined_sections(mine):
        theirs = shifted(mine, "s", 1)
        return jnp.where(first, mine, theirs), jnp.where(first, theirs, mine)

    def pieces_round_z(block):
        return [block] + [shifted(block, "z", k) for k in range(1, 4)]

    def vectors_of(pieces):
        parts = [piece[at, SHARE:] for piece, at in pieces]
        ordered = []
        for shard in range(4):
            pick = parts[3]
            for k in range(3):
                pick = jnp.where(z == (shard + k) % 4, parts[k], pick)
            ordered.append(pick.reshape(-1))
        whole_vectors = jnp.stack(ordered)
        at, members = 0, []
        for width in (192, 192, 192, 192, 576, 192, 768, 192):
            members.append(whole_vectors[:, at : at + width].reshape(1, -1).astype(F32))
            at += width
        head = [lax.dynamic_slice_in_dim(members[4], t * D + unit * HD, HD, 1) for t in range(3)]
        units = [lax.dynamic_slice_in_dim(members[6], t * D + unit * 48, 48, 1) for t in range(4)]
        return (
            jnp.concatenate(members[:4] + [jnp.zeros((4, D), F32)], 0),
            jnp.concatenate(
                [jnp.concatenate(head, 1), jnp.concatenate(units, 1), jnp.zeros((6, UNITS), F32)], 0
            ),
            members[5] + members[7],
        )

    early = joined_sections(shares[0])
    early = after(n_sent, early)
    layer_share = [[(piece, 0) for piece in pieces_round_z(early[0][None])]]
    later = joined_sections(after(early, shares[1]))

    blk = ROWS // 2
    offsets = jnp.arange(SEQ, dtype=jnp.int32)
    blocks = after(early, blocks)
    row_blocks = jnp.where(first, blocks[0], blocks[1])
    places = (jnp.repeat(row_blocks, blk) * blk + offsets % blk).reshape(8, 2, ROWS)
    places = jnp.where(c == 0, places, places[:, ::-1]).transpose(1, 0, 2).reshape(SEQ)
    half = ROT // 2
    frequencies = 10000.0 ** (-jnp.arange(half, dtype=F32) * 2.0 / ROT)
    angles = places.astype(F32)[:, None] * frequencies[None, :]
    cos, sin = jnp.cos(angles), jnp.sin(angles)
    none = jnp.zeros((SEQ, half), F32)
    still = jnp.zeros((SEQ, HD - ROT), F32)
    cosine = jnp.concatenate([cos, cos, still + 1.0] * 2, 1)
    ahead = jnp.concatenate([-sin, none, still] * 2, 1)
    behind = jnp.concatenate([none, sin, still] * 2, 1)
    order = row_blocks.reshape(8, 2, 2)
    order = jnp.where(c == 0, order, order[:, ::-1]).transpose(1, 0, 2).reshape(SEQ // BLK)
    tables = (cosine, ahead, behind)
    own, (tables, layer_share[0]) = exchanged(
        n_sent, (tables, [piece for piece, _ in layer_share[0]])
    )
    layer_share[0] = [(piece, 0) for piece in layer_share[0]]
    layer_vectors = [vectors_of(layer_share[0])]
    normals = both_cores(own)
    place = jnp.stack([z.astype(jnp.int32), owner])

    kept = []
    for l in range(LAYERS):
        own, other, qkv, pre, act = call(
            forward_kernel,
            [((HALF, D), BF), ((HALF, D), BF), ((SEQ, UNITS), BF), ((SEQ, UNITS), F32), ((SEQ, 256), BF)],
            place, order, *normals, layer_vectors[l][0], layer_vectors[l][1], *layer_share[l], *tables,
            scratch=WEIGHT_SCRATCH + (VMEM((SEQ, HD), BF),), smem=2, room=56, takes=11,
        )
        if l == 1:
            sent = after(normals, jnp.broadcast_to(dx[None], (8, ROWS, D)))
            branches, (own, other) = exchanged(sent, (own, other))
            branches = both_cores(branches)
        kept.append((x, normals, qkv, pre, act))
        if l + 1 < LAYERS:
            joined = halves_joined(own, other)
            if l == 0:
                block = jnp.stack([later[0], early[1], later[1]])
                pieces = pieces_round_z(after(layer_share[0], block))
                joined, pieces[1], pieces[3] = lax.optimization_barrier((joined, pieces[1], pieces[3]))
            got = exchanged(joined)
            x, n_sent = call(
                functools.partial(finish_kernel, l == 1),
                [((ROWS, D), F32), ((8, ROWS, D), BF)], got, x, layer_vectors[l][2],
            )
            if l == 0:
                own, pieces = exchanged(n_sent, pieces)
                layer_share += [[(piece, i) for piece in pieces] for i in range(3)]
                layer_vectors += [vectors_of(share) for share in layer_share[1:]]
                normals = both_cores(own)
            else:
                normals = both_cores(exchanged(n_sent))
    last = halves_joined(own, other)

    dx = dx.astype(F32)
    packs, shares = [None] * LAYERS, [None] * LAYERS
    def sent_round(pack):
        parts = [lax.dynamic_index_in_dim(pack, (z + k) % 4, 0, False) for k in range(4)]
        return [parts[0]] + [shifted(parts[k], "z", k) for k in range(1, 4)]

    def summed(parts):
        return sum(part.astype(F32) for part in parts).astype(BF)

    def both_sections(j):
        mine = jnp.where(first, shares[j], shares[j + 2])
        theirs = shifted(jnp.where(first, shares[j + 2], shares[j]), "s", 1)
        return (mine.astype(F32) + theirs.astype(F32)).astype(BF)

    for l in reversed(range(LAYERS)):
        x, normals, qkv, pre, act = kept[l]
        own, other, d_qkv, d_up, sums = call(
            backward_kernel,
            [((HALF, D), BF), ((HALF, D), BF), ((SEQ, UNITS), BF), ((SEQ, UNITS), BF), ((8, D), F32)],
            place, order, *branches, *normals, layer_vectors[l][0], *layer_share[l], *tables, qkv, pre,
            scratch=WEIGHT_SCRATCH + (VMEM((SEQ, HD), F32),) * 3 + (VMEM((SEQ, HD), BF),), smem=2, room=56, takes=13,
        )
        if l + 1 == LAYERS:
            got, (own, other) = exchanged(last, (own, other))
            final = call(
                functools.partial(finish_kernel, False),
                [((ROWS, D), F32), ((8, ROWS, D), BF)], got, x, layer_vectors[l][2],
            )[0]
        else:
            own, other, parts = lax.optimization_barrier((own, other, parts))
            shares[l + 1] = summed(parts)
        pack = call(
            product_kernel, [((4, PACK, 384), BF)],
            *branches, *normals, layer_vectors[l][0], act, d_qkv, d_up, sums,
            scratch=(VMEM((D, UNITS), F32), VMEM((D, UNITS), F32), VMEM((256, D), F32)),
            room=56, takes=6,
        )[0]
        got, pack = exchanged(halves_joined(own, other), pack)
        dx, branch_sent = call(
            functools.partial(finish_back_kernel, l == 2),
            [((ROWS, D), F32), ((8, ROWS, D), BF)], got, x, dx,
        )
        if l > 0:
            parts = sent_round(pack)
            branches, parts[2] = exchanged(branch_sent, parts[2])
            branches = both_cores(branches)

    sent = jnp.broadcast_to(after(got, both_sections(1))[None], (8, PACK, 384))
    shares[0] = summed(sent_round(pack))
    own, initial = exchanged(sent, (both_sections(0), dx))
    initial, dx = initial

    corner = jnp.stack([c, z]).astype(jnp.int32)
    earlier = unpacked(1, corner, own, shifted(own, "c", 1), ())
    sent = jnp.broadcast_to(initial[None], (8, PACK, 384))
    came = shifted(jnp.where(first, final, dx), "s", 1)
    own, (earlier, came) = exchanged(sent, (earlier, came))
    grad_qkv, grad_out, grad_up, grad_down, extra = unpacked(
        0, corner, own, shifted(own, "c", 1), earlier
    )
    norm_sums = jnp.sum(extra[:, :, 0:2], 1)
    v_g1, v_h1 = norm_sums[:, 0, :192], norm_sums[:, 0, 192:]
    v_g2, v_h2 = norm_sums[:, 1, :192], norm_sums[:, 1, 192:]
    v_qkv = extra[:, :H, 2, :192].reshape(2, H, 3, HD).transpose(0, 2, 1, 3).reshape(2, 3 * D)
    v_qkv = lax.dynamic_slice_in_dim(v_qkv, z * 576, 576, 1)
    v_up = extra[:, :, 2, 192:].reshape(2, 16, 4, 48).transpose(0, 2, 1, 3).reshape(2, 4, D)
    v_up = lax.dynamic_index_in_dim(v_up, z, 1, False)
    v_branch = extra[:, 0, 3, :192]

    have = jnp.where(first, dx, final)
    boundary = jnp.stack([jnp.where(first, have, came), jnp.where(first, came, have)])
    boundary = boundary.reshape(1, 2, 1, ROWS, D)
    return (
        boundary, v_g1, v_h1, v_g2, v_h2, grad_qkv, v_qkv, grad_out, v_branch,
        grad_up, v_up, grad_down, v_branch,
    )


def solution(mesh):
    wide = Mesh(mesh.devices.reshape(2, 2, 4, 2, 4), EVERY)
    acts = P("s", None, "z", CTX, None)
    vec = P("s", "z")
    mat = P("s", "z", None)
    placed = (acts, P(), vec, vec, vec, vec, mat, vec, mat, vec, mat, vec, mat, vec)
    outs = (acts, vec, vec, vec, vec, mat, vec, mat, vec, mat, vec, mat, vec)
    return jax.shard_map(body, mesh=wide, in_specs=placed, out_specs=outs, check_vma=False)
```

```python
import functools

import jax
import jax.numpy as jnp
from jax import lax
from jax.experimental import pallas as pl
from jax.experimental.pallas import tpu as pltpu
from jax.sharding import Mesh, PartitionSpec as P

D = 768
H = 12
HD = 64
FF = 3072
ROT = 16
LAYERS = 4
EPSILON = 1e-05
SCORE_SCALE = 0.125
CHIPS = ("xh", "y")
CTX = ("xh", "y", "c")
EVERY = ("s", "xh", "y", "c", "z")
BF = jnp.bfloat16
F32 = jnp.float32
ROWS = 64
SEQ = 1024
HALF = SEQ // 2
BLOCK = 256
BLK = 32
UNITS = 192
SHARE = 416
PACK = 432
VMEM = pltpu.VMEM
MIB = 1024 * 1024


def shifted(block, axis, distance):
    size = lax.axis_size(axis)
    return lax.ppermute(block, axis, [(i, (i + distance) % size) for i in range(size)])


def dot(left, right, left_dim=1, right_dim=0):
    return lax.dot_general(
        left, right, (((left_dim,), (right_dim,)), ((), ())), preferred_element_type=F32
    )


def cost(microseconds):
    return pl.CostEstimate(
        flops=int(microseconds * 1e9), bytes_accessed=int(microseconds * 3.5e6), transcendentals=0
    )


def whole(shape):
    return pl.BlockSpec(shape, lambda _: (0,) * len(shape))


def call(kernel, outs, *args, scratch=(), smem=0, room=12, takes=2):
    specs = [pl.BlockSpec(memory_space=pltpu.SMEM)] * smem
    for i in range(smem, len(args)):
        if isinstance(args[i], tuple):
            block, at = args[i]
            if block.shape[0] == 8:
                specs.append(pl.BlockSpec((8, ROWS, D), lambda _, at=at: (0, at, 0)))
            else:
                specs.append(pl.BlockSpec((None,) + block.shape[1:], lambda _, at=at: (at, 0, 0)))
        else:
            specs.append(whole(args[i].shape))
    args = [a[0] if isinstance(a, tuple) else a for a in args]
    return pl.pallas_call(
        kernel,
        out_shape=[jax.ShapeDtypeStruct(shape, dtype) for shape, dtype in outs],
        in_specs=specs,
        out_specs=[whole(shape) for shape, _ in outs],
        grid=(1,),
        scratch_shapes=list(scratch),
        cost_estimate=cost(takes),
        compiler_params=pltpu.CompilerParams(vmem_limit_bytes=room * MIB),
    )(*args)


def centred(x):
    offset = x - jnp.mean(x, -1, keepdims=True)
    scale = lax.rsqrt(jnp.mean(offset * offset, -1, keepdims=True) + EPSILON)
    return offset * scale, scale


def start_kernel(x, cotangent, out):
    n = centred(x[...])[0].astype(BF)
    for k in range(8):
        out[k, 0:ROWS] = n
        out[k, ROWS:] = cotangent[...]


def rows_of(source, step):
    count = BLOCK // ROWS
    return source[pl.ds(step * count, count)].reshape(BLOCK, D)


def finish_kernel(rounded, got, x, bias, x_out, n_out):
    total = got[0].astype(F32)
    for k in range(1, 8):
        total = total + got[k].astype(F32)
    x_next = x[...] + (total + bias[...])
    if rounded:
        x_next = x_next.astype(BF).astype(F32)
    x_out[...] = x_next
    n = centred(x_next)[0].astype(BF)
    for k in range(8):
        n_out[k] = n


def finish_back_kernel(rounded, got, x, dx, dx_out, branch_out):
    gy = got[0].astype(F32)
    for k in range(1, 8):
        gy = gy + got[k].astype(F32)
    n, scale = centred(x[...])
    inner = jnp.mean(gy * n, -1, keepdims=True)
    dx_next = dx[...] + scale * (gy - jnp.mean(gy, -1, keepdims=True) - n * inner)
    if rounded:
        dx_next = dx_next.astype(BF).astype(F32)
    dx_out[...] = dx_next
    branch = dx_next.astype(BF)
    for k in range(8):
        branch_out[k] = branch


def share_weights(place, pieces, w_qkv, w_up, w_both):
    for k, piece in enumerate(pieces):
        at = lax.rem(place[0] + (4 - k), 4)
        w_qkv[pl.ds(pl.multiple_of(at * 192, 64), 192), :] = piece[0:192, 0:192]
        w_up[pl.ds(pl.multiple_of(at * 192, 64), 192), :] = piece[0:192, 192:384]
        w_both[pl.ds(pl.multiple_of(at * 48, 16), 48), 0:384] = piece[192:240, :]
        w_both[pl.ds(pl.multiple_of(at * 48, 16), 48), 384:768] = piece[304:352, :]

        @pl.when(at == place[1])
        def _():
            w_both[192:256, 0:384] = piece[240:304, :]
            w_both[192:256, 384:768] = piece[352:416, :]


WEIGHT_SCRATCH = (VMEM((D, UNITS), BF), VMEM((D, UNITS), BF), VMEM((UNITS + HD, D), BF))


def scored(tile, q, k):
    scores = dot(q * SCORE_SCALE, k, 1, 1)
    row = lax.broadcasted_iota(jnp.int32, (BLOCK, BLOCK), 0)
    column = lax.broadcasted_iota(jnp.int32, (BLOCK, BLOCK), 1)
    last = jnp.where(row >= column, scores[:, tile * BLOCK :], -1e30)
    if tile:
        last = jnp.concatenate([scores[:, : tile * BLOCK], last], 1)
    raised = jnp.exp(last - jnp.max(last, -1, keepdims=True))
    return raised * (1.0 / jnp.sum(raised, -1, keepdims=True))


def spots(order, half, step):
    for i in range(BLOCK // BLK):
        at = order[half * (HALF // BLK) + step * (BLOCK // BLK) + i]
        yield i * BLK, pl.ds(pl.multiple_of(at * BLK, BLK), BLK)


def turn(v, tables, rows, sign):
    cosine, ahead, behind = tables
    return v * cosine[rows, :] + sign * (
        pltpu.roll(v, 120, 1) * ahead[rows, :] + pltpu.roll(v, 8, 1) * behind[rows, :]
    )


def forward_kernel(
    place, order, own, other, vec, bias, s0, s1, s2, s3, cosine, ahead, behind,
    part_own, part_other, qkv, pre, act,
    w_qkv, w_up, w_both, att,
):
    share_weights(place, (s0, s1, s2, s3), w_qkv, w_up, w_both)
    tables = (cosine, ahead, behind)
    for half, source in enumerate((own, other)):

        @pl.loop(0, HALF // BLOCK)
        def _(step):
            rows = pl.ds(half * HALF + step * BLOCK, BLOCK)
            n = rows_of(source, step).astype(F32)
            one = (n * vec[0:1, :] + vec[1:2, :]).astype(BF)
            two = (n * vec[2:3, :] + vec[3:4, :]).astype(BF)
            merged = dot(one, w_qkv[...]) + bias[0:1, 0:192]
            qk = turn(merged[:, 0:128], tables, rows, 1.0).astype(BF)
            v = merged[:, 128:192].astype(BF)
            for at, spot in spots(order, half, step):
                qkv[spot, 0:128] = qk[at : at + BLK, :]
                qkv[spot, 128:192] = v[at : at + BLK, :]
            up = dot(two, w_up[...]) + bias[1:2, 0:192]
            pre[rows, :] = up
            act[rows, 0:192] = (0.5 * up * (1.0 + lax.erf(up * 0.7071067811865476))).astype(BF)

    for tile in range(SEQ // BLOCK):
        start, end = tile * BLOCK, (tile + 1) * BLOCK
        probs = scored(tile, qkv[start:end, 0:64], qkv[0:end, 64:128]).astype(BF)
        att[start:end, :] = dot(probs, qkv[0:end, 128:192]).astype(BF)

    for half, target in enumerate((part_own, part_other)):

        @pl.loop(0, HALF // BLOCK)
        def _(step):
            rows = pl.ds(half * HALF + step * BLOCK, BLOCK)
            attended = jnp.concatenate([att[spot, :] for _, spot in spots(order, half, step)], 0)
            act[rows, 192:256] = attended
            target[pl.ds(step * BLOCK, BLOCK), :] = dot(act[rows, :], w_both[...]).astype(BF)


def backward_kernel(
    place, order, b_own, b_other, n_own, n_other, vec, s0, s1, s2, s3, cosine, ahead, behind, qkv, pre,
    gy_own, gy_other, d_qkv, d_up, sums,
    w_qkv, w_up, w_both, dq, dk, dv, grad,
):
    share_weights(place, (s0, s1, s2, s3), w_qkv, w_up, w_both)
    tables = (cosine, ahead, behind)
    sums[...] = jnp.zeros_like(sums)
    for half, source in enumerate((b_own, b_other)):

        @pl.loop(0, HALF // BLOCK)
        def _(step):
            rows = pl.ds(half * HALF + step * BLOCK, BLOCK)
            branch = rows_of(source, step)
            sums[5:6, :] += jnp.sum(branch.astype(F32), 0, keepdims=True)
            both = dot(branch, w_both[...], 1, 1)
            up = pre[rows, :]
            slope = 0.5 * (1.0 + lax.erf(up * 0.7071067811865476)) + up * (
                jnp.exp(-0.5 * up * up) * 0.3989422804014327
            )
            d_up[rows, :] = (slope * both[:, 0:192]).astype(BF)
            head = both[:, 192:256].astype(BF)
            for at, spot in spots(order, half, step):
                grad[spot, :] = head[at : at + BLK, :]

    for tile in reversed(range(SEQ // BLOCK)):
        start, end = tile * BLOCK, (tile + 1) * BLOCK
        q, k, v = qkv[start:end, 0:64], qkv[0:end, 64:128], qkv[0:end, 128:192]
        out = grad[start:end, :]
        probs = scored(tile, q, k)
        prob_grad = dot(out, v, 1, 1)
        inner = jnp.sum(probs * prob_grad, -1, keepdims=True)
        score_grad = (probs * (prob_grad - inner)).astype(BF)
        dq[start:end, :] = dot(score_grad, k)
        k_part, v_part = dot(score_grad, q, 0, 0), dot(probs.astype(BF), out, 0, 0)
        if end == SEQ:
            dk[...] = k_part
            dv[...] = v_part
        else:
            dk[0:end, :] += k_part
            dv[0:end, :] += v_part

    for half, (source, target) in enumerate(((n_own, gy_own), (n_other, gy_other))):

        @pl.loop(0, HALF // BLOCK)
        def _(step):
            here = pl.ds(step * BLOCK, BLOCK)
            rows = pl.ds(half * HALF + step * BLOCK, BLOCK)
            places = [spot for _, spot in spots(order, half, step)]
            both = jnp.concatenate(
                [jnp.concatenate([ref[spot, :] for spot in places], 0) for ref in (dq, dk)], 1
            )
            d_qkv[rows, 0:128] = turn(both * SCORE_SCALE, tables, rows, -1.0).astype(BF)
            d_qkv[rows, 128:192] = jnp.concatenate([dv[spot, :] for spot in places], 0).astype(BF)
            g_qkv, g_up = d_qkv[rows, :], d_up[rows, :]
            one = dot(g_qkv, w_qkv[...], 1, 1)
            two = dot(g_up, w_up[...], 1, 1)
            target[here, :] = (one * vec[0:1, :] + two * vec[2:3, :]).astype(BF)
            n = rows_of(source, step).astype(F32)
            for at, part in enumerate((one * n, one, two * n, two)):
                sums[at : at + 1, :] += jnp.sum(part, 0, keepdims=True)
            sums[4:5, 0:192] += jnp.sum(g_qkv.astype(F32), 0, keepdims=True)
            sums[6:7, 0:192] += jnp.sum(g_up.astype(F32), 0, keepdims=True)


def product_kernel(b_own, b_other, n_own, n_other, vec, act, d_qkv, d_up, sums, pack, in_qkv, in_up, in_act):
    in_qkv[...] = jnp.zeros_like(in_qkv)
    in_up[...] = jnp.zeros_like(in_up)
    in_act[...] = jnp.zeros_like(in_act)
    for half, (branch, normal) in enumerate(((b_own, n_own), (b_other, n_other))):

        @pl.loop(0, HALF // BLOCK)
        def _(step):
            rows = pl.ds(half * HALF + step * BLOCK, BLOCK)
            n = rows_of(normal, step).astype(F32)
            one = (n * vec[0:1, :] + vec[1:2, :]).astype(BF)
            two = (n * vec[2:3, :] + vec[3:4, :]).astype(BF)
            in_qkv[...] += dot(one, d_qkv[rows, :], 0, 0)
            in_up[...] += dot(two, d_up[rows, :], 0, 0)
            in_act[...] += dot(act[rows, :], rows_of(branch, step), 0, 0)

    blank = jnp.zeros((12, 384), F32)
    out = in_act[192:256, :].astype(BF)
    for z in range(4):
        pack[z, 0:192, 0:192] = in_qkv[z * 192 : (z + 1) * 192, :].astype(BF)
        pack[z, 0:192, 192:384] = in_up[z * 192 : (z + 1) * 192, :].astype(BF)
        down = in_act[z * 48 : (z + 1) * 48, :].astype(BF)
        pack[z, 192:240, :] = down[:, 0:384]
        pack[z, 240:304, :] = out[:, 0:384]
        pack[z, 304:352, :] = down[:, 384:768]
        pack[z, 352:416, :] = out[:, 384:768]
        cut = sums[:, z * 192 : (z + 1) * 192]
        left = jnp.concatenate([cut[0:1], cut[2:3], sums[4:5, 0:192], cut[5:6]], 0)
        right = jnp.concatenate([cut[1:2], cut[3:4], sums[6:7, 0:192], jnp.zeros((1, 192), F32)], 0)
        rows = jnp.concatenate([left, right], 1)
        pack[z, 416:432, :] = jnp.concatenate([rows, blank], 0).astype(BF)


def unpack_kernel(place, own, other, *refs):
    g_qkv, g_out, g_up, g_down, rest = refs[-5:]
    low = place[0] == 0
    z = place[1]
    for i in range(16):
        k = i // 2
        mine, theirs = (own, other) if i % 2 == 0 else (other, own)
        block = jnp.where(low, mine[k], theirs[k]).astype(F32)
        if i < H:
            for t in range(3):
                g_qkv[0, :, t * D + i * HD : t * D + (i + 1) * HD] = block[0:192, t * HD : (t + 1) * HD]
        for t in range(4):
            at = t * D + i * 48
            g_up[0, :, at : at + 48] = block[0:192, 192 + t * 48 : 240 + t * 48]
        g_down[0, i * 48 : (i + 1) * 48, 0:384] = block[192:240, :]
        g_down[0, i * 48 : (i + 1) * 48, 384:768] = block[304:352, :]
        rest[0, i] = block[416:432, :]
    for h in range(3):
        i = 3 * z + h
        k = i // 2
        mine = (i % 2) == place[0]
        out = jnp.where(mine, own[k], other[k]).astype(F32)
        g_out[0, h * HD : (h + 1) * HD, 0:384] = out[240:304, :]
        g_out[0, h * HD : (h + 1) * HD, 384:768] = out[352:416, :]


UNPACKED = ((192, 3 * D), (192, D), (192, FF), (D, D), (16, 16, 384))


def unpacked(j, place, own, other, earlier):
    specs = [pl.BlockSpec(memory_space=pltpu.SMEM)]
    specs += [pl.BlockSpec((8, PACK, 384), lambda i: (0, 0, 0))] * 2
    specs += [pl.BlockSpec(memory_space=pl.ANY)] * len(earlier)
    return pl.pallas_call(
        unpack_kernel,
        grid=(1,),
        out_shape=[jax.ShapeDtypeStruct((2,) + shape, F32) for shape in UNPACKED],
        in_specs=specs,
        out_specs=[
            pl.BlockSpec((1,) + shape, lambda i, n=len(shape): (j,) + (0,) * n) for shape in UNPACKED
        ],
        input_output_aliases={3 + i: i for i in range(len(earlier))},
        cost_estimate=cost(7),
        compiler_params=pltpu.CompilerParams(vmem_limit_bytes=56 * MIB),
    )(place, own, other, *earlier)


def after(earlier, later):
    return lax.optimization_barrier((earlier, later))[1]


def body(ends, blocks, g1, h1, g2, h2, wq, bq, wo, bo, wu, bu, wd, bd):
    s = lax.axis_index("s")
    c = lax.axis_index("c")
    z = lax.axis_index("z")
    first = s == 0
    unit = lax.axis_index(CTX)
    has_head = unit < H
    owner = jnp.minimum(unit // 3, 3).astype(jnp.int32)

    keep = jnp.where(first, ends[0, 0, 0], ends[0, 1, 0])
    received = shifted(jnp.where(first, ends[0, 1, 0], ends[0, 0, 0]), "s", 1)
    x = jnp.where(first, keep, received).astype(F32)
    dx = jnp.where(first, received, keep)

    def exchanged(sent, beside=None):
        got = lax.all_to_all(sent, CHIPS, 0, 0, tiled=True)
        return got if beside is None else lax.optimization_barrier((got, beside))

    def both_cores(own):
        return own, shifted(own, "c", 1)

    def halves_joined(own, other):
        return (own + shifted(other, "c", 1)).reshape(8, ROWS, D)

    n_sent = call(start_kernel, [((8, 2 * ROWS, D), BF)], x, dx)[0]
    mask = has_head.astype(BF)

    def cut(w, at, sizes):
        return lax.dynamic_slice(w, at, sizes)

    zero = jnp.int32(0)
    cols = [cut(wq, (zero, zero, t * D + unit * HD), (2, 192, HD)) * mask for t in range(3)]
    cols += [cut(wu, (zero, zero, t * D + unit * 48), (2, 192, 48)) for t in range(4)]
    down = cut(wd, (zero, unit * 48, zero), (2, 48, D))
    out = cut(wo, (zero, (unit % 3) * HD, zero), (2, HD, D)) * mask
    rows = jnp.concatenate([down, out], 1)
    vectors = jnp.concatenate([g1, h1, g2, h2, bq, bo, bu, bd], 1)
    vectors = jnp.pad(vectors, ((0, 0), (0, 16 * 384 - vectors.shape[1]))).reshape(2, 16, 384)
    shares = jnp.concatenate(
        [jnp.concatenate(cols, 2), rows[..., :384], rows[..., 384:], vectors], 1
    )

    def joined_sections(mine):
        theirs = shifted(mine, "s", 1)
        return jnp.where(first, mine, theirs), jnp.where(first, theirs, mine)

    def pieces_round_z(block):
        return [block] + [shifted(block, "z", k) for k in range(1, 4)]

    def vectors_of(pieces):
        parts = [piece[at, SHARE:] for piece, at in pieces]
        ordered = []
        for shard in range(4):
            pick = parts[3]
            for k in range(3):
                pick = jnp.where(z == (shard + k) % 4, parts[k], pick)
            ordered.append(pick.reshape(-1))
        whole_vectors = jnp.stack(ordered)
        at, members = 0, []
        for width in (192, 192, 192, 192, 576, 192, 768, 192):
            members.append(whole_vectors[:, at : at + width].reshape(1, -1).astype(F32))
            at += width
        head = [lax.dynamic_slice_in_dim(members[4], t * D + unit * HD, HD, 1) for t in range(3)]
        units = [lax.dynamic_slice_in_dim(members[6], t * D + unit * 48, 48, 1) for t in range(4)]
        return (
            jnp.concatenate(members[:4] + [jnp.zeros((4, D), F32)], 0),
            jnp.concatenate(
                [jnp.concatenate(head, 1), jnp.concatenate(units, 1), jnp.zeros((6, UNITS), F32)], 0
            ),
            members[5] + members[7],
        )

    early = joined_sections(shares[0])
    early = after(n_sent, early)
    layer_share = [[(piece, 0) for piece in pieces_round_z(early[0][None])]]
    later = joined_sections(after(early, shares[1]))

    blk = ROWS // 2
    offsets = jnp.arange(SEQ, dtype=jnp.int32)
    blocks = after(early, blocks)
    row_blocks = jnp.where(first, blocks[0], blocks[1])
    places = (jnp.repeat(row_blocks, blk) * blk + offsets % blk).reshape(8, 2, ROWS)
    places = jnp.where(c == 0, places, places[:, ::-1]).transpose(1, 0, 2).reshape(SEQ)
    half = ROT // 2
    frequencies = 10000.0 ** (-jnp.arange(half, dtype=F32) * 2.0 / ROT)
    angles = places.astype(F32)[:, None] * frequencies[None, :]
    cos, sin = jnp.cos(angles), jnp.sin(angles)
    none = jnp.zeros((SEQ, half), F32)
    still = jnp.zeros((SEQ, HD - ROT), F32)
    cosine = jnp.concatenate([cos, cos, still + 1.0] * 2, 1)
    ahead = jnp.concatenate([-sin, none, still] * 2, 1)
    behind = jnp.concatenate([none, sin, still] * 2, 1)
    order = row_blocks.reshape(8, 2, 2)
    order = jnp.where(c == 0, order, order[:, ::-1]).transpose(1, 0, 2).reshape(SEQ // BLK)
    tables = (cosine, ahead, behind)
    own, (tables, layer_share[0]) = exchanged(
        n_sent, (tables, [piece for piece, _ in layer_share[0]])
    )
    layer_share[0] = [(piece, 0) for piece in layer_share[0]]
    layer_vectors = [vectors_of(layer_share[0])]
    started = both_cores(own)
    normals = [(rows, 0) for rows in started]
    branches = [(rows, 1) for rows in started]
    place = jnp.stack([z.astype(jnp.int32), owner])

    kept = []
    for l in range(LAYERS):
        own, other, qkv, pre, act = call(
            forward_kernel,
            [((HALF, D), BF), ((HALF, D), BF), ((SEQ, UNITS), BF), ((SEQ, UNITS), F32), ((SEQ, 256), BF)],
            place, order, *normals, layer_vectors[l][0], layer_vectors[l][1], *layer_share[l], *tables,
            scratch=WEIGHT_SCRATCH + (VMEM((SEQ, HD), BF),), smem=2, room=56, takes=11,
        )
        kept.append((x, normals, qkv, pre, act))
        if l + 1 < LAYERS:
            joined = halves_joined(own, other)
            if l == 0:
                block = jnp.stack([later[0], early[1], later[1]])
                pieces = pieces_round_z(after(layer_share[0], block))
                joined, pieces[1], pieces[3] = lax.optimization_barrier((joined, pieces[1], pieces[3]))
            got = exchanged(joined)
            x, n_sent = call(
                functools.partial(finish_kernel, l == 1),
                [((ROWS, D), F32), ((8, ROWS, D), BF)], got, x, layer_vectors[l][2],
            )
            if l == 0:
                own, pieces = exchanged(n_sent, pieces)
                layer_share += [[(piece, i) for piece in pieces] for i in range(3)]
                layer_vectors += [vectors_of(share) for share in layer_share[1:]]
                normals = both_cores(own)
            else:
                normals = both_cores(exchanged(n_sent))
    last = halves_joined(own, other)

    dx = dx.astype(F32)
    packs, shares = [None] * LAYERS, [None] * LAYERS
    def sent_round(pack):
        parts = [lax.dynamic_index_in_dim(pack, (z + k) % 4, 0, False) for k in range(4)]
        return [parts[0]] + [shifted(parts[k], "z", k) for k in range(1, 4)]

    def summed(parts):
        return sum(part.astype(F32) for part in parts).astype(BF)

    def both_sections(j):
        mine = jnp.where(first, shares[j], shares[j + 2])
        theirs = shifted(jnp.where(first, shares[j + 2], shares[j]), "s", 1)
        return (mine.astype(F32) + theirs.astype(F32)).astype(BF)

    for l in reversed(range(LAYERS)):
        x, normals, qkv, pre, act = kept[l]
        own, other, d_qkv, d_up, sums = call(
            backward_kernel,
            [((HALF, D), BF), ((HALF, D), BF), ((SEQ, UNITS), BF), ((SEQ, UNITS), BF), ((8, D), F32)],
            place, order, *branches, *normals, layer_vectors[l][0], *layer_share[l], *tables, qkv, pre,
            scratch=WEIGHT_SCRATCH + (VMEM((SEQ, HD), F32),) * 3 + (VMEM((SEQ, HD), BF),), smem=2, room=56, takes=13,
        )
        if l + 1 == LAYERS:
            got, (own, other) = exchanged(last, (own, other))
            final = call(
                functools.partial(finish_kernel, False),
                [((ROWS, D), F32), ((8, ROWS, D), BF)], got, x, layer_vectors[l][2],
            )[0]
        pack = call(
            product_kernel, [((4, PACK, 384), BF)],
            *branches, *normals, layer_vectors[l][0], act, d_qkv, d_up, sums,
            scratch=(VMEM((D, UNITS), F32), VMEM((D, UNITS), F32), VMEM((256, D), F32)),
            room=56, takes=6,
        )[0]
        joined = halves_joined(own, other)
        if l + 1 < LAYERS:
            joined, parts = lax.optimization_barrier((joined, parts))
            shares[l + 1] = summed(parts)
        got, pack = exchanged(joined, pack)
        dx, branch_sent = call(
            functools.partial(finish_back_kernel, l == 2),
            [((ROWS, D), F32), ((8, ROWS, D), BF)], got, x, dx,
        )
        if l > 0:
            parts = sent_round(pack)
            branches, parts[2] = exchanged(branch_sent, parts[2])
            branches = both_cores(branches)

    sent = jnp.broadcast_to(after(got, both_sections(1))[None], (8, PACK, 384))
    shares[0] = summed(sent_round(pack))
    own, initial = exchanged(sent, (both_sections(0), dx))
    initial, dx = initial

    corner = jnp.stack([c, z]).astype(jnp.int32)
    earlier = unpacked(1, corner, own, shifted(own, "c", 1), ())
    sent = jnp.broadcast_to(initial[None], (8, PACK, 384))
    came = shifted(jnp.where(first, final, dx), "s", 1)
    own, (earlier, came) = exchanged(sent, (earlier, came))
    grad_qkv, grad_out, grad_up, grad_down, extra = unpacked(
        0, corner, own, shifted(own, "c", 1), earlier
    )
    norm_sums = jnp.sum(extra[:, :, 0:2], 1)
    v_g1, v_h1 = norm_sums[:, 0, :192], norm_sums[:, 0, 192:]
    v_g2, v_h2 = norm_sums[:, 1, :192], norm_sums[:, 1, 192:]
    v_qkv = extra[:, :H, 2, :192].reshape(2, H, 3, HD).transpose(0, 2, 1, 3).reshape(2, 3 * D)
    v_qkv = lax.dynamic_slice_in_dim(v_qkv, z * 576, 576, 1)
    v_up = extra[:, :, 2, 192:].reshape(2, 16, 4, 48).transpose(0, 2, 1, 3).reshape(2, 4, D)
    v_up = lax.dynamic_index_in_dim(v_up, z, 1, False)
    v_branch = extra[:, 0, 3, :192]

    have = jnp.where(first, dx, final)
    boundary = jnp.stack([jnp.where(first, have, came), jnp.where(first, came, have)])
    boundary = boundary.reshape(1, 2, 1, ROWS, D)
    return (
        boundary, v_g1, v_h1, v_g2, v_h2, grad_qkv, v_qkv, grad_out, v_branch,
        grad_up, v_up, grad_down, v_branch,
    )


def solution(mesh):
    wide = Mesh(mesh.devices.reshape(2, 2, 4, 2, 4), EVERY)
    acts = P("s", None, "z", CTX, None)
    vec = P("s", "z")
    mat = P("s", "z", None)
    placed = (acts, P(), vec, vec, vec, vec, mat, vec, mat, vec, mat, vec, mat, vec)
    outs = (acts, vec, vec, vec, vec, mat, vec, mat, vec, mat, vec, mat, vec)
    return jax.shard_map(body, mesh=wide, in_specs=placed, out_specs=outs, check_vma=False)
```
